32 devices in a mesh: case: 2 (over y), brick: 4 (over z), sect: 2 (over x), slab: 2 (over core).
Axes of the slice: x: 2, y: 2, z: 4, core: 2. Of those that a mesh axis runs over, the one named last changes fastest.
Arguments:
- geometry: bfloat16 [64, 32, 32, 128], P(None, ('case', 'brick'), ('sect', 'slab')), parts along dimension 1, may hold values from -6 to 6
- conv_kernels: bfloat16 [1, 3, 3, 3, 64, 64], replicated, may hold values from -0.15625 to 0.15625
- point_place: float32 [3, 8192], P(None, ('case', 'brick', 'sect', 'slab')), parts along dimension 1, may hold values from 0 to 1
- point_attr: bfloat16 [8192, 64], P(('case', 'brick', 'sect', 'slab')), parts along dimension 0, may hold values from -6 to 6
- destination: int32 [8192, 1], P(('case', 'brick', 'sect', 'slab')), parts along dimension 0, may hold values from 0 to 7; in each aligned block of 256 rows (0 to 255, 256 to 511, ...) at most 40 rows name the same one
- dense_first: bfloat16 [2, 128, 512], replicated, may hold values from -1 to 1
- dense_middle: bfloat16 [2, 3, 512, 512], replicated, may hold values from -0.5 to 0.5
- dense_last: bfloat16 [2, 4, 512], replicated, may hold values from -0.25 to 0.25
Outputs:
- prediction: float32 [4, 10240], P(None, ('case', 'brick', 'sect', 'slab')), parts along dimension 1
The draws below stay inside these ranges and needn't reach their ends.
There are 2 independent parts, one for each index of `case`. The reference program is written for one: setup_inputs(seed, part) draws one part's arguments, and reference() takes and returns one part's arrays. A program takes and returns all parts, laid end to end along the dimension named above; an argument that names none is the same for every part. Nothing has to cross between parts.
Inputs may be any that keep to these rules, and one draw needn't show every extreme that they name: A destination names a brick index and a sect index as brick * 2 + sect; its sect index fixes the point's section. No destination is named by more than 40 of the points of one device, and some device names some destination exactly 40 times.
All inputs are finite; a program needn't handle non-finite values.
Results may differ from the reference program's by a relative error of at most 0.0075.
Values may be sent and summed in bfloat16 or wider, within the bound.
A program may use at most 64 MiB of HBM per device.

```python
import math
import jax
import jax.numpy as jnp
import numpy as np
from jax import lax

C = 64
ATTR = 64
HID = 512
OUTC = 4
NMID = 3
NCONV = 1
BX = 4
BY = 8
GZ = 128
PTS_DEV = 256
F = 128
CAP = 40
BUF = 320
GX = 16
GY = 32
PTS = 4096
ROWS = 5120
N_BRICK = 4
N_SECT = 2
N_SLAB = 2


def steps_of(rng, dims, cuts, low, high):
    def one(dim, shards_of):
        steps = jax.random.uniform(jax.random.fold_in(jax.random.fold_in(rng, 6), dim), (shards_of,), jnp.float32, low / len(cuts), high / len(cuts))
        return jnp.repeat(jnp.exp(steps), dims[dim] // shards_of).reshape((-1,) + (1,) * (len(dims) - dim - 1))

    gain = one(*cuts[0])
    for cut in cuts[1:]:
        gain = gain * one(*cut)
    return gain


def deal_out(rng, own, number, rows, number_of, top, bound, skew):
    order = jax.random.permutation(rng, number_of)
    crowded, common = load_shares(number_of, rows * top, bound, skew, True), load_shares(number_of, rows * top, bound, skew, False)
    places = jnp.arange(number_of)

    def named(lengths, offset_by):
        used = int((lengths > 0).sum())
        fixed = max(1, used // 4)
        shifted = fixed + (places - fixed + offset_by * (used - fixed)) % max(1, number_of - fixed)
        return jnp.zeros((number_of,), jnp.int32).at[order[jnp.where(places < fixed, places, shifted)]].set(jnp.asarray(lengths, jnp.int32))

    lengths = jnp.where(number % 4 == 0, named(crowded, number // 4), named(common, number - number // 4 - 1))
    mixed = jax.random.permutation(jax.random.fold_in(own, 3), number_of)
    giver, receiver = mixed[0:number_of // 2 * 2:2], mixed[1:number_of // 2 * 2:2]
    slack = jnp.minimum(lengths[giver] - 1, bound - lengths[receiver]) // 2
    slack = jnp.where((giver == order[0]) | (receiver == order[0]) | (lengths[receiver] == 0), 0, jnp.maximum(slack, 0))
    shifted = jax.random.randint(jax.random.fold_in(own, 4), (number_of // 2,), 0, 1 << 20) % (slack + 1)
    lengths = lengths.at[giver].add(-shifted).at[receiver].add(shifted)
    items = jnp.searchsorted(jnp.cumsum(lengths), jnp.arange(rows * top), side="right").astype(jnp.int32)
    listing = items.reshape(top, rows).T
    listing = listing[jax.random.permutation(jax.random.fold_in(own, 1), rows)]
    offset_by = jax.random.randint(jax.random.fold_in(own, 2), (rows, 1), 0, top)
    return jnp.take_along_axis(listing, (jnp.arange(top)[None, :] + offset_by) % top, axis=1)


def load_shares(count, total, bound, slope, full):
    portions = [(1 << 20) // math.isqrt(rank ** slope) + 1 for rank in range(1, count + 1)]
    largest = bound if full else min(bound, max(-(-total // count), total * portions[0] // sum(portions)))
    least = 1 if total - largest >= count - 1 else 0
    counts, spare = [largest] + [least] * (count - 1), total - largest - least * (count - 1)
    while spare > 0:
        movable = [i for i in range(1, count) if counts[i] < largest] or [i for i in range(1, count) if counts[i] < bound]
        whole, left = sum([portions[i] for i in movable]), spare
        for i in movable:
            extra = min(bound - counts[i], max(1, left * portions[i] // whole), spare)
            counts[i] = counts[i] + extra
            spare = spare - extra
    return np.array(counts)


def noise(own_key, shape, spread, most, shards=(), kind=jnp.bfloat16):
    loudness = steps_of(own_key, shape, shards, -0.22, 0.18) if shards else 1.0
    array = jax.random.normal(own_key, shape, jnp.float32) * spread * loudness
    return jnp.minimum(jnp.maximum(array, -most), most).astype(kind)


def setup_inputs(seed: int = 0, part: int = 0) -> dict:
    streams_of = jax.random.split(jax.random.key(seed), 9)
    part_splits = jax.random.split(jax.random.fold_in(streams_of[8], part), 9)
    geometry = noise(part_splits[0], (C, GX, GY, GZ), 1.0, 6.0, ((1, 4), (2, 4)))
    conv_kernels = noise(streams_of[1], (NCONV, 3, 3, 3, C, C), (27 * C) ** -0.5, 0.15625)
    point_place = jnp.clip(1.0 * jax.random.uniform(part_splits[2], (3, PTS), jnp.float32) ** steps_of(part_splits[2], (3, PTS), ((1, 16),), -0.2, 0.2), 0.0, 1.0)
    point_attr = noise(part_splits[3], (PTS, ATTR), 1.0, 6.0, ((0, 16),))
    destination_keys = jax.random.split(jax.random.fold_in(part_splits[4], 1), PTS // PTS_DEV)
    destination_turns = jax.random.permutation(jax.random.fold_in(part_splits[4], 3), PTS // PTS_DEV)
    destination = jax.vmap(lambda own, number: deal_out(jax.random.fold_in(part_splits[4], 2), own, number, PTS_DEV, N_BRICK * N_SECT, 1, CAP, 2))(destination_keys, destination_turns).reshape((PTS, 1))
    dense_first = noise(streams_of[5], (2, F, HID), (F // 4) ** -0.5, 1.0)
    dense_middle = noise(streams_of[6], (2, NMID, HID, HID), (HID // 4) ** -0.5, 0.5)
    dense_last = noise(streams_of[7], (2, OUTC, HID), HID ** -0.5, 0.25)
    return {"geometry": geometry, "conv_kernels": conv_kernels, "point_place": point_place, "point_attr": point_attr, "destination": destination, "dense_first": dense_first, "dense_middle": dense_middle, "dense_last": dense_last}


def convolve(features_now, kernel):
    response = lax.conv_general_dilated(features_now[None], kernel, (1, 1, 1), ((1, 1), (1, 1), (1, 1)), dimension_numbers=("NCDHW", "DHWIO", "NCDHW"), preferred_element_type=jnp.float32)
    return response[0]


def hat(offset):
    return jnp.maximum(0.0, 1.0 - jnp.abs(offset))


def network(table_rows, first_weights, middle_weights, last_weights):
    activity = jax.nn.gelu(jnp.dot(table_rows, first_weights, preferred_element_type=jnp.float32), approximate=True).astype(jnp.bfloat16)
    for ordinal in range(NMID):
        activity = jax.nn.gelu(jnp.dot(activity, middle_weights[ordinal], preferred_element_type=jnp.float32), approximate=True).astype(jnp.bfloat16)
    return lax.dot_general(last_weights, activity, (((1,), (1,)), ((), ())), preferred_element_type=jnp.float32)


def reference(geometry, conv_kernels, point_place, point_attr, destination, dense_first, dense_middle, dense_last):
    features_now = geometry
    for ordinal in range(NCONV):
        response = convolve(features_now, conv_kernels[ordinal])
        features_now = (features_now.astype(jnp.float32) + jax.nn.gelu(response, approximate=True)).astype(jnp.bfloat16)
    padded = jnp.pad(features_now, ((0, 0), (1, 1), (1, 1), (1, 1)))
    owner = jnp.arange(PTS, dtype=jnp.int32) // PTS_DEV
    brick_of = owner // (N_SECT * N_SLAB)
    column_of = owner % (N_SECT * N_SLAB)
    local_x = point_place[0] * BX
    local_y = point_place[1] * BY
    local_z = point_place[2] * GZ
    base_x = jnp.floor(local_x - 0.5).astype(jnp.int32)
    base_y = jnp.floor(local_y - 0.5).astype(jnp.int32)
    base_z = jnp.floor(local_z - 0.5).astype(jnp.int32)
    feature = jnp.zeros((C, PTS), jnp.float32)
    for shift_x in (0, 1):
        cell_x = base_x + shift_x
        weight_x = hat(local_x - (cell_x.astype(jnp.float32) + 0.5))
        for shift_y in (0, 1):
            cell_y = base_y + shift_y
            weight_y = hat(local_y - (cell_y.astype(jnp.float32) + 0.5))
            for shift_z in (0, 1):
                cell_z = base_z + shift_z
                rounded_z = lax.optimization_barrier(hat(local_z - (cell_z.astype(jnp.float32) + 0.5)).astype(jnp.bfloat16))
                weight_z = rounded_z.astype(jnp.float32)
                values = padded[:, brick_of * BX + cell_x + 1, column_of * BY + cell_y + 1, cell_z + 1].astype(jnp.float32)
                feature = feature + values * (weight_z * weight_x * weight_y)
    feature = feature.T.astype(jnp.bfloat16)
    table_rows = jnp.concatenate([feature, point_attr], axis=1)
    target = destination[:, 0]
    blocked = target.reshape(PTS // PTS_DEV, PTS_DEV)
    targets_all = jnp.arange(N_BRICK * N_SECT, dtype=jnp.int32)
    onehot = (blocked[:, :, None] == targets_all[None, None, :]).astype(jnp.int32)
    before = (jnp.cumsum(onehot, axis=1) - onehot).astype(jnp.int32)
    arrival = jnp.sum(before * onehot, axis=2).astype(jnp.int32).reshape(PTS)
    slot_index = (target * N_SLAB + owner % N_SLAB) * BUF + (owner // N_SLAB) * CAP + arrival
    upper = (target % N_SECT) >= (N_SECT // 2)
    surface_value = network(table_rows, dense_first[0], dense_middle[0], dense_last[0])
    volume_value = network(table_rows, dense_first[1], dense_middle[1], dense_last[1])
    chosen = jnp.where(upper[None, :], volume_value, surface_value)
    prediction = jnp.zeros((OUTC, ROWS), jnp.float32).at[:, slot_index.astype(jnp.int32)].set(chosen)
    return prediction
```

```python
import functools

import jax
import jax.numpy as jnp
from jax import lax
from jax.experimental import pallas as pl
from jax.experimental.pallas import tpu as pltpu
from jax.sharding import PartitionSpec as P

MESH = pl.DeviceIdType.MESH
DIRECTIONS = ((1, 0), (-1, 0), (1, 1), (1, -1), (-1, 1), (-1, -1), (0, 1), (0, -1))
NT = (((1,), (1,)), ((), ()))


def hat(offset):
    return jnp.maximum(0.0, 1.0 - jnp.abs(offset))


def gelu(value):
    return jax.nn.gelu(value, approximate=True)


def dot(a, b):
    return jnp.dot(a, b, preferred_element_type=jnp.float32)


def send_range(step, size):
    return {1: pl.ds(size, 1), -1: pl.ds(1, 1), 0: pl.ds(1, size)}[step]


def land_range(step, size):
    return {1: pl.ds(0, 1), -1: pl.ds(size + 1, 1), 0: pl.ds(1, size)}[step]


def kernel(
    bricks,
    sects,
    slabs,
    geometry,
    kernels,
    place,
    attr,
    target,
    first,
    middle,
    last,
    out,
    geo,
    wide,
    pad,
    lat,
    taps,
    taps_t,
    first_v,
    middle_v,
    outbox,
    inbox,
    local_sem,
    send_sem,
    recv_sem,
    value_send,
    value_recv,
):
    channels, span_x, span_y, span_z = geo.shape
    count = place.shape[1]
    peers = bricks * sects
    cap = 5 * count // (4 * peers)
    half = peers // 2 * cap
    brick = lax.axis_index("brick")
    sect = lax.axis_index("sect")
    slab = lax.axis_index("slab")
    column = sect * slabs + slab
    columns = sects * slabs
    me = brick * sects + sect
    linear = me * slabs + slab
    everyone = peers * slabs

    barrier = pltpu.get_barrier_semaphore()
    for j in range(1, everyone):
        other = lax.rem(linear + j, everyone)
        pl.semaphore_signal(
            barrier,
            inc=1,
            device_id={
                "brick": other // columns,
                "sect": other % columns // slabs,
                "slab": other % slabs,
            },
            device_id_type=MESH,
        )

    loads = [
        pltpu.make_async_copy(geometry, geo, local_sem.at[0]),
        pltpu.make_async_copy(kernels, taps, local_sem.at[1]),
        pltpu.make_async_copy(first, first_v, local_sem.at[2]),
        pltpu.make_async_copy(middle, middle_v, local_sem.at[3]),
    ]
    for load in loads:
        load.start()

    loads[0].wait()
    for x in range(span_x):
        wide[...] = geo[:, x].astype(jnp.float32).reshape(channels * span_y, span_z)
        for y in range(span_y):
            pad[x + 1, y + 1] = wide[pl.ds(y, channels, stride=span_y), :].astype(jnp.bfloat16)

    def inside(dx, dy):
        b, c = brick + dx, column + dy
        return (b >= 0) & (b < bricks) & (c >= 0) & (c < columns)

    def halo_copy(buffer, phase, k):
        dx, dy = DIRECTIONS[k]
        c = column + dy
        return pltpu.make_async_remote_copy(
            src_ref=buffer.at[send_range(dx, span_x), send_range(dy, span_y)],
            dst_ref=buffer.at[land_range(dx, span_x), land_range(dy, span_y)],
            send_sem=send_sem.at[phase, k],
            recv_sem=recv_sem.at[phase, k],
            device_id={"brick": brick + dx, "sect": c // slabs, "slab": c % slabs},
            device_id_type=MESH,
        )

    def start(buffer, phase, which):
        for k in which:
            @pl.when(inside(*DIRECTIONS[k]))
            def _():
                halo_copy(buffer, phase, k).start()

    def land(buffer, phase, which):
        for k in which:
            dx, dy = DIRECTIONS[k]

            @pl.when(inside(-dx, -dy))
            def _():
                halo_copy(buffer, phase, k).wait_recv()

    def drain(buffer, phase):
        for k in range(8):
            @pl.when(inside(*DIRECTIONS[k]))
            def _():
                halo_copy(buffer, phase, k).wait_send()

    pl.semaphore_wait(barrier, everyone - 1)
    start(pad, 0, range(8))

    for k, (dx, dy) in enumerate(DIRECTIONS):
        @pl.when(jnp.logical_not(inside(-dx, -dy)))
        def _():
            for buffer in (pad, lat):
                region = buffer.at[land_range(dx, span_x), land_range(dy, span_y)]
                region[...] = jnp.zeros(region.shape, jnp.bfloat16)

    loads[1].wait()
    for a in range(3):
        for b in range(3):
            for e in range(3):
                tap = taps[0, a, b, e].astype(jnp.float32).T.astype(jnp.bfloat16)
                taps_t[a, e * channels:(e + 1) * channels, b * channels:(b + 1) * channels] = tap

    local_x = place[0:1, :] * span_x
    local_y = place[1:2, :] * span_y
    local_z = place[2:3, :] * span_z
    cells = lax.broadcasted_iota(jnp.int32, (span_z, count), 0).astype(jnp.float32)
    weight_z = hat(local_z - (cells + 0.5)).astype(jnp.bfloat16)
    weight_x = [hat(local_x - (x - 0.5)) for x in range(span_x + 2)]
    weight_y = [hat(local_y - (y - 0.5)) for y in range(span_y + 2)]

    named = lax.broadcasted_iota(jnp.int32, (peers, count), 0)
    onehot = named == target[...]
    earlier = lax.broadcasted_iota(jnp.int32, (count, count), 0) < lax.broadcasted_iota(
        jnp.int32, (count, count), 1
    )
    before = dot(onehot.astype(jnp.bfloat16), earlier.astype(jnp.bfloat16))
    named_brick = lax.div(named, jnp.int32(sects))
    named_sect = named - named_brick * sects
    upper = (named_sect >= sects // 2).astype(jnp.int32)
    block = upper * (peers // 2) + named_brick * (sects // 2) + named_sect - upper * (sects // 2)
    position = jnp.sum(
        jnp.where(onehot, before + (block * cap).astype(jnp.float32), 0.0), axis=0, keepdims=True
    )
    slots = lax.broadcasted_iota(jnp.int32, (2 * half, count), 0)
    gather = (slots == position.astype(jnp.int32)).astype(jnp.bfloat16)

    lane = lax.broadcasted_iota(jnp.int32, (channels, span_z), 1)

    def conv_row(x):
        total = None
        for a in range(3):
            near = jnp.concatenate(
                [pad[x + a, y:y + 3].reshape(3 * channels, span_z) for y in range(span_y)], axis=1
            )
            term = dot(taps_t[a], near)
            total = term if total is None else total + term
        for y in range(span_y):
            part = total[:, y * span_z:(y + 1) * span_z]
            left = pltpu.roll(part[:channels], 1, 1)
            right = pltpu.roll(part[2 * channels:], span_z - 1, 1)
            response = (
                part[channels:2 * channels]
                + jnp.where(lane == 0, 0.0, left)
                + jnp.where(lane == span_z - 1, 0.0, right)
            )
            old = pad[x + 1, y + 1].astype(jnp.float32)
            lat[x + 1, y + 1] = (old + gelu(response)).astype(jnp.bfloat16)

    land(pad, 0, (6, 7))
    for x in range(1, span_x - 1):
        conv_row(x)
    land(pad, 0, range(6))
    conv_row(0)
    conv_row(span_x - 1)
    start(lat, 1, range(8))

    def sample(total, x, low, high):
        part = dot(lat[x, low:high].reshape((high - low) * channels, span_z), weight_z)
        inner = None
        for y in range(low, high):
            term = part[(y - low) * channels:(y - low + 1) * channels] * weight_y[y]
            inner = term if inner is None else inner + term
        inner = inner * weight_x[x]
        return inner if total is None else total + inner

    total = None
    for x in range(1, span_x + 1):
        total = sample(total, x, 1, span_y + 1)
    land(lat, 1, (6, 7))
    for x in range(1, span_x + 1):
        total = sample(total, x, 0, 1)
        total = sample(total, x, span_y + 1, span_y + 2)
    land(lat, 1, range(6))
    for x in (0, span_x + 1):
        total = sample(total, x, 0, span_y + 2)
    row = jnp.concatenate([total.astype(jnp.bfloat16), attr[...]], axis=0)
    table = lax.dot_general(gather, row, NT, preferred_element_type=jnp.float32)
    table = table.astype(jnp.bfloat16)

    loads[2].wait()
    loads[3].wait()
    outbox[...] = jnp.zeros(outbox.shape, jnp.float32)
    for s in range(2):
        act = gelu(dot(table[s * half:(s + 1) * half], first_v[s])).astype(jnp.bfloat16)
        for layer in range(middle.shape[1]):
            act = gelu(dot(act, middle_v[s, layer])).astype(jnp.bfloat16)
        value = lax.dot_general(last[s], act, NT, preferred_element_type=jnp.float32)
        outbox[s, 0:value.shape[0], 0:half] = value

    def value_copy(j):
        other = lax.rem(me + j, peers)
        there = other % sects
        return pltpu.make_async_remote_copy(
            src_ref=outbox.at[there // (sects // 2)],
            dst_ref=inbox.at[me],
            send_sem=value_send.at[j],
            recv_sem=value_recv.at[j],
            device_id={"brick": other // sects, "sect": there},
            device_id_type=MESH,
        )

    for j in range(1, peers):
        value_copy(j).start()
    inbox[me] = outbox[sect // (sects // 2)]
    drain(pad, 0)
    drain(lat, 1)
    for j in range(1, peers):
        value_copy(j).wait()

    width = inbox.shape[2]
    own = (brick * (sects // 2) + sect % (sects // 2)) * cap
    rolled = pltpu.roll(inbox[...].reshape(peers * 8, width), lax.rem(width - own, width), 1)
    for i in range(peers):
        out[:, i * cap:(i + 1) * cap] = rolled[i * 8:i * 8 + out.shape[0], 0:cap]


def on_device(
    sizes,
    geometry,
    conv_kernels,
    point_place,
    point_attr,
    destination,
    dense_first,
    dense_middle,
    dense_last,
):
    bricks, sects, slabs = sizes
    channels, span_x, span_y, span_z = geometry.shape
    count = point_place.shape[1]
    peers = bricks * sects
    cap = 5 * count // (4 * peers)
    width = -(-(peers // 2 * cap) // 128) * 128
    padded = (span_x + 2, span_y + 2, channels, span_z)
    anywhere = pl.BlockSpec(memory_space=pl.ANY)
    local = pl.BlockSpec(memory_space=pltpu.VMEM)
    return pl.pallas_call(
        functools.partial(kernel, bricks, sects, slabs),
        out_shape=jax.ShapeDtypeStruct((dense_last.shape[1], peers * cap), jnp.float32),
        in_specs=[anywhere, anywhere, local, local, local, anywhere, anywhere, local],
        out_specs=local,
        scratch_shapes=[
            pltpu.VMEM(geometry.shape, jnp.bfloat16),
            pltpu.VMEM((channels * span_y, span_z), jnp.float32),
            pltpu.VMEM(padded, jnp.bfloat16),
            pltpu.VMEM(padded, jnp.bfloat16),
            pltpu.VMEM(conv_kernels.shape, jnp.bfloat16),
            pltpu.VMEM((3, 3 * channels, 3 * channels), jnp.bfloat16),
            pltpu.VMEM(dense_first.shape, jnp.bfloat16),
            pltpu.VMEM(dense_middle.shape, jnp.bfloat16),
            pltpu.VMEM((2, 8, width), jnp.float32),
            pltpu.VMEM((peers, 8, width), jnp.float32),
            pltpu.SemaphoreType.DMA((4,)),
            pltpu.SemaphoreType.DMA((2, 8)),
            pltpu.SemaphoreType.DMA((2, 8)),
            pltpu.SemaphoreType.DMA((peers,)),
            pltpu.SemaphoreType.DMA((peers,)),
        ],
        compiler_params=pltpu.CompilerParams(
            collective_id=0, has_side_effects=True, vmem_limit_bytes=48 * 2**20
        ),
    )(
        geometry,
        conv_kernels,
        point_place,
        point_attr.T,
        destination.reshape(1, count),
        dense_first,
        dense_middle,
        dense_last,
    )


def solution(mesh):
    sizes = tuple(mesh.shape[axis] for axis in ("brick", "sect", "slab"))
    in_specs = (
        P(None, ("case", "brick"), ("sect", "slab"), None),
        P(),
        P(None, ("case", "brick", "sect", "slab")),
        P(("case", "brick", "sect", "slab"), None),
        P(("case", "brick", "sect", "slab"), None),
        P(),
        P(),
        P(),
    )
    out_specs = P(None, ("case", "brick", "sect", "slab"))
    return jax.shard_map(
        functools.partial(on_device, sizes),
        mesh=mesh,
        in_specs=in_specs,
        out_specs=out_specs,
        check_vma=False,
    )
```

```python
import functools
import math

import jax
import jax.numpy as jnp
from jax import lax
from jax.experimental import pallas as pl
from jax.experimental.pallas import tpu as pltpu
from jax.sharding import PartitionSpec as P

MESH = pl.DeviceIdType.MESH
DIRECTIONS = ((1, 0), (-1, 0), (1, 1), (1, -1), (-1, 1), (-1, -1), (0, 1), (0, -1))
NT = (((1,), (1,)), ((), ()))


def hat(offset):
    return jnp.maximum(0.0, 1.0 - jnp.abs(offset))


def gelu(value):
    scale = (2.0 / math.pi) ** 0.5
    middle = 0.5 * value
    return middle + middle * jnp.tanh(value * (scale + (scale * 0.044715) * (value * value)))


def dot(a, b):
    return jnp.dot(a, b, preferred_element_type=jnp.float32)


def send_range(step, size):
    return {1: pl.ds(size, 1), -1: pl.ds(1, 1), 0: pl.ds(1, size)}[step]


def land_range(step, size):
    return {1: pl.ds(0, 1), -1: pl.ds(size + 1, 1), 0: pl.ds(1, size)}[step]


def kernel(
    bricks,
    sects,
    slabs,
    geometry,
    kernels,
    place_in,
    attr_in,
    target_in,
    first,
    middle,
    last_in,
    out,
    geo,
    wide,
    pad,
    lat,
    taps,
    taps_t,
    place,
    attr,
    target,
    first_v,
    middle_v,
    last,
    near_place,
    partial,
    incoming,
    outbox,
    inbox,
    local_sem,
    send_sem,
    recv_sem,
    value_send,
    value_recv,
):
    channels, span_x, span_y, span_z = geo.shape
    count = place.shape[1]
    peers = bricks * sects
    cap = 5 * count // (4 * peers)
    half = peers // 2 * cap
    brick = lax.axis_index("brick")
    sect = lax.axis_index("sect")
    slab = lax.axis_index("slab")
    column = sect * slabs + slab
    columns = sects * slabs
    me = brick * sects + sect
    linear = me * slabs + slab
    everyone = peers * slabs

    loads = [
        pltpu.make_async_copy(source, landing, local_sem.at[i])
        for i, (source, landing) in enumerate(
            (
                (geometry, geo),
                (place_in, place),
                (kernels, taps),
                (target_in, target),
                (attr_in, attr),
                (first, first_v),
                (middle, middle_v),
                (last_in, last),
            )
        )
    ]
    for load in loads:
        load.start()

    barrier = pltpu.get_barrier_semaphore()
    for j in range(1, everyone):
        other = lax.rem(linear + j, everyone)
        pl.semaphore_signal(
            barrier,
            inc=1,
            device_id={
                "brick": other // columns,
                "sect": other % columns // slabs,
                "slab": other % slabs,
            },
            device_id_type=MESH,
        )

    def inside(dx, dy):
        b, c = brick + dx, column + dy
        return (b >= 0) & (b < bricks) & (c >= 0) & (c < columns)

    def remote(source, landing, phase, k):
        dx, dy = DIRECTIONS[k]
        c = column + dy
        return pltpu.make_async_remote_copy(
            src_ref=source,
            dst_ref=landing,
            send_sem=send_sem.at[phase, k],
            recv_sem=recv_sem.at[phase, k],
            device_id={"brick": brick + dx, "sect": c // slabs, "slab": c % slabs},
            device_id_type=MESH,
        )

    def halo_copy(phase, k):
        dx, dy = DIRECTIONS[k]
        if phase == 1 and dy == 0:
            return remote(partial.at[k], incoming.at[k], phase, k)
        if phase == 2:
            return remote(place, near_place.at[k], phase, k)
        buffer = (pad, lat)[phase]
        return remote(
            buffer.at[send_range(dx, span_x), send_range(dy, span_y)],
            buffer.at[land_range(dx, span_x), land_range(dy, span_y)],
            phase,
            k,
        )

    def start(phase, which):
        for k in which:
            @pl.when(inside(*DIRECTIONS[k]))
            def _():
                halo_copy(phase, k).start()

    def land(phase, which):
        for k in which:
            dx, dy = DIRECTIONS[k]

            @pl.when(inside(-dx, -dy))
            def _():
                halo_copy(phase, k).wait_recv()

    def drain(phase, which):
        for k in which:
            @pl.when(inside(*DIRECTIONS[k]))
            def _():
                halo_copy(phase, k).wait_send()

    def turn(x):
        base = x * channels * span_y
        wide[base:base + channels * span_y] = (
            geo[:, x].astype(jnp.float32).reshape(channels * span_y, span_z)
        )
        for y in range(span_y):
            pad[x + 1, y + 1] = wide[pl.ds(base + y, channels, stride=span_y), :].astype(
                jnp.bfloat16
            )

    loads[0].wait()
    turn(0)
    turn(span_x - 1)
    loads[1].wait()
    pl.semaphore_wait(barrier, everyone - 1)
    start(0, range(6))
    start(2, (0, 1))
    for x in range(1, span_x - 1):
        turn(x)
    start(0, (6, 7))

    for k, (dx, dy) in enumerate(DIRECTIONS):
        @pl.when(jnp.logical_not(inside(-dx, -dy)))
        def _():
            for buffer in (pad, lat):
                region = buffer.at[land_range(dx, span_x), land_range(dy, span_y)]
                region[...] = jnp.zeros(region.shape, jnp.bfloat16)
            if dy == 0:
                near_place[k] = jnp.zeros(near_place.shape[1:], jnp.float32)
                incoming[k] = jnp.zeros(incoming.shape[1:], jnp.bfloat16)

    loads[2].wait()
    for a in range(3):
        for b in range(3):
            for e in range(3):
                tap = taps[0, a, b, e].astype(jnp.float32).T.astype(jnp.bfloat16)
                low = (a * 3 + b) * channels
                taps_t[e * channels:(e + 1) * channels, low:low + channels] = tap

    cells = lax.broadcasted_iota(jnp.int32, (span_z, count), 0).astype(jnp.float32) + 0.5

    def weights(points):
        local_x = points[0:1, :] * span_x
        local_y = points[1:2, :] * span_y
        local_z = points[2:3, :] * span_z
        return (
            [hat(local_x - (x - 0.5)) for x in range(span_x + 2)],
            [hat(local_y - (y - 0.5)) for y in range(span_y + 2)],
            hat(local_z - cells).astype(jnp.bfloat16),
        )

    own_weights = weights(place)

    loads[3].wait()
    named = lax.broadcasted_iota(jnp.int32, (peers, count), 0)
    onehot = named == target[...]
    earlier = lax.broadcasted_iota(jnp.int32, (count, count), 0) < lax.broadcasted_iota(
        jnp.int32, (count, count), 1
    )
    before = dot(onehot.astype(jnp.bfloat16), earlier.astype(jnp.bfloat16))
    named_brick = lax.div(named, jnp.int32(sects))
    named_sect = named - named_brick * sects
    upper = (named_sect >= sects // 2).astype(jnp.int32)
    block = upper * (peers // 2) + named_brick * (sects // 2) + named_sect - upper * (sects // 2)
    position = jnp.sum(
        jnp.where(onehot, before + (block * cap).astype(jnp.float32), 0.0), axis=0, keepdims=True
    )
    slots = lax.broadcasted_iota(jnp.int32, (2 * half, count), 0)
    gather = (slots == position.astype(jnp.int32)).astype(jnp.bfloat16)

    lane = lax.broadcasted_iota(jnp.int32, (channels, span_z), 1)

    def product(x, y, low, high):
        near = jnp.concatenate(
            [
                jnp.concatenate(
                    [pad[x + a, y + i:y + i + 3].reshape(3 * channels, span_z) for i in (0, 1)],
                    axis=1,
                )
                for a in range(low, high)
            ],
            axis=0,
        )
        return dot(taps_t[:, low * 3 * channels:high * 3 * channels], near)

    def finish(x, y, pair):
        for i in (0, 1):
            part = pair[:, i * span_z:(i + 1) * span_z]
            left = pltpu.roll(part[:channels], 1, 1)
            right = pltpu.roll(part[2 * channels:], span_z - 1, 1)
            response = (
                part[channels:2 * channels]
                + jnp.where(lane == 0, 0.0, left)
                + jnp.where(lane == span_z - 1, 0.0, right)
            )
            old = pad[x + 1, y + i + 1].astype(jnp.float32)
            lat[x + 1, y + i + 1] = (old + gelu(response)).astype(jnp.bfloat16)

    land(0, (6, 7))
    for x in range(1, span_x - 1):
        for y in range(0, span_y, 2):
            finish(x, y, product(x, y, 0, 3))
    early = [
        [product(x, y, low, high) for y in range(0, span_y, 2)]
        for x, low, high in ((0, 1, 3), (span_x - 1, 0, 2))
    ]
    land(0, range(6))
    for side, (x, a) in enumerate(((0, 0), (span_x - 1, 2))):
        for y in range(0, span_y, 2):
            finish(x, y, early[side][y // 2] + product(x, y, a, a + 1))
    start(1, range(2, 8))

    def sample(of_weights, x, weight, low, high):
        weight_y, weight_z = of_weights[1:]
        part = dot(lat[x, low:high].reshape((high - low) * channels, span_z), weight_z)
        inner = None
        for y in range(low, high):
            term = part[(y - low) * channels:(y - low + 1) * channels] * weight_y[y]
            inner = term if inner is None else inner + term
        return inner * weight

    land(2, (0, 1))
    for k, x, weight in ((0, span_x, 0), (1, 1, span_x + 1)):
        theirs = weights(near_place.at[1 - k])
        partial[k] = sample(theirs, x, theirs[0][weight], 1, span_y + 1).astype(jnp.bfloat16)
    start(1, (0, 1))

    weight_x = own_weights[0]
    total = None
    for x in range(1, span_x + 1):
        term = sample(own_weights, x, weight_x[x], 1, span_y + 1)
        total = term if total is None else total + term
    land(1, range(2, 8))
    for x in range(span_x + 2):
        total = total + sample(own_weights, x, weight_x[x], 0, 1)
        total = total + sample(own_weights, x, weight_x[x], span_y + 1, span_y + 2)
    for load in loads[4:]:
        load.wait()
    land(1, (0, 1))
    total = total + incoming[0].astype(jnp.float32) + incoming[1].astype(jnp.float32)
    row = jnp.concatenate([total.astype(jnp.bfloat16), attr[...]], axis=0)
    table = lax.dot_general(gather, row, NT, preferred_element_type=jnp.float32)
    table = table.astype(jnp.bfloat16)

    acts = [
        gelu(dot(table[s * half:(s + 1) * half], first_v[s])).astype(jnp.bfloat16) for s in range(2)
    ]
    for layer in range(middle_v.shape[1]):
        acts = [gelu(dot(acts[s], middle_v[s, layer])).astype(jnp.bfloat16) for s in range(2)]
    outbox[...] = jnp.zeros(outbox.shape, jnp.float32)
    for s in range(2):
        value = lax.dot_general(last[s], acts[s], NT, preferred_element_type=jnp.float32)
        outbox[s, 0:value.shape[0], 0:half] = value

    def value_copy(j):
        other = lax.rem(me + j, peers)
        there = other % sects
        return pltpu.make_async_remote_copy(
            src_ref=outbox.at[there // (sects // 2)],
            dst_ref=inbox.at[me],
            send_sem=value_send.at[j],
            recv_sem=value_recv.at[j],
            device_id={"brick": other // sects, "sect": there},
            device_id_type=MESH,
        )

    for j in range(1, peers):
        value_copy(j).start()
    inbox[me] = outbox[sect // (sects // 2)]
    drain(0, range(8))
    drain(1, range(8))
    drain(2, (0, 1))
    for j in range(1, peers):
        value_copy(j).wait()

    width = inbox.shape[2]
    own = (brick * (sects // 2) + sect % (sects // 2)) * cap
    rolled = pltpu.roll(inbox[...].reshape(peers * 8, width), lax.rem(width - own, width), 1)
    for i in range(peers):
        out[:, i * cap:(i + 1) * cap] = rolled[i * 8:i * 8 + out.shape[0], 0:cap]


def on_device(
    sizes,
    geometry,
    conv_kernels,
    point_place,
    point_attr,
    destination,
    dense_first,
    dense_middle,
    dense_last,
):
    bricks, sects, slabs = sizes
    channels, span_x, span_y, span_z = geometry.shape
    count = point_place.shape[1]
    peers = bricks * sects
    cap = 5 * count // (4 * peers)
    width = -(-(peers // 2 * cap) // 128) * 128
    padded = (span_x + 2, span_y + 2, channels, span_z)
    attr = point_attr.T
    target = destination.reshape(1, count)
    return pl.pallas_call(
        functools.partial(kernel, bricks, sects, slabs),
        out_shape=jax.ShapeDtypeStruct((dense_last.shape[1], peers * cap), jnp.float32),
        in_specs=[pl.BlockSpec(memory_space=pl.ANY)] * 8,
        out_specs=pl.BlockSpec(memory_space=pltpu.VMEM),
        scratch_shapes=[
            pltpu.VMEM(geometry.shape, jnp.bfloat16),
            pltpu.VMEM((span_x * channels * span_y, span_z), jnp.float32),
            pltpu.VMEM(padded, jnp.bfloat16),
            pltpu.VMEM(padded, jnp.bfloat16),
            pltpu.VMEM(conv_kernels.shape, jnp.bfloat16),
            pltpu.VMEM((3 * channels, 9 * channels), jnp.bfloat16),
            pltpu.VMEM(point_place.shape, jnp.float32),
            pltpu.VMEM(attr.shape, jnp.bfloat16),
            pltpu.VMEM(target.shape, jnp.int32),
            pltpu.VMEM(dense_first.shape, jnp.bfloat16),
            pltpu.VMEM(dense_middle.shape, jnp.bfloat16),
            pltpu.VMEM(dense_last.shape, jnp.bfloat16),
            pltpu.VMEM((2,) + point_place.shape, jnp.float32),
            pltpu.VMEM((2, channels, count), jnp.bfloat16),
            pltpu.VMEM((2, channels, count), jnp.bfloat16),
            pltpu.VMEM((2, 8, width), jnp.float32),
            pltpu.VMEM((peers, 8, width), jnp.float32),
            pltpu.SemaphoreType.DMA((8,)),
            pltpu.SemaphoreType.DMA((3, 8)),
            pltpu.SemaphoreType.DMA((3, 8)),
            pltpu.SemaphoreType.DMA((peers,)),
            pltpu.SemaphoreType.DMA((peers,)),
        ],
        compiler_params=pltpu.CompilerParams(
            collective_id=0, has_side_effects=True, vmem_limit_bytes=60 * 2**20
        ),
    )(
        geometry,
        conv_kernels,
        point_place,
        attr,
        target,
        dense_first,
        dense_middle,
        dense_last,
    )


def solution(mesh):
    sizes = tuple(mesh.shape[axis] for axis in ("brick", "sect", "slab"))
    in_specs = (
        P(None, ("case", "brick"), ("sect", "slab"), None),
        P(),
        P(None, ("case", "brick", "sect", "slab")),
        P(("case", "brick", "sect", "slab"), None),
        P(("case", "brick", "sect", "slab"), None),
        P(),
        P(),
        P(),
    )
    out_specs = P(None, ("case", "brick", "sect", "slab"))
    return jax.shard_map(
        functools.partial(on_device, sizes),
        mesh=mesh,
        in_specs=in_specs,
        out_specs=out_specs,
        check_vma=False,
    )
```

```python
import functools
import math

import jax
import jax.numpy as jnp
from jax import lax
from jax.experimental import pallas as pl
from jax.experimental.pallas import tpu as pltpu
from jax.sharding import PartitionSpec as P

MESH = pl.DeviceIdType.MESH
DIRECTIONS = ((1, 0), (-1, 0), (1, 1), (1, -1), (-1, 1), (-1, -1), (0, 1), (0, -1))
NT = (((1,), (1,)), ((), ()))


def hat(offset):
    return jnp.maximum(0.0, 1.0 - jnp.abs(offset))


def gelu(value):
    scale = (2.0 / math.pi) ** 0.5
    middle = 0.5 * value
    return middle + middle * jnp.tanh(value * (scale + (scale * 0.044715) * (value * value)))


def dot(a, b):
    return jnp.dot(a, b, preferred_element_type=jnp.float32)


def send_range(step, size):
    return {1: pl.ds(size, 1), -1: pl.ds(1, 1), 0: pl.ds(1, size)}[step]


def land_range(step, size):
    return {1: pl.ds(0, 1), -1: pl.ds(size + 1, 1), 0: pl.ds(1, size)}[step]


def kernel(
    bricks,
    sects,
    slabs,
    geometry,
    kernels,
    place_in,
    attr_in,
    target_in,
    first,
    middle,
    last_in,
    out,
    geo,
    wide,
    pad,
    lat,
    taps,
    taps_t,
    place,
    attr,
    target,
    first_v,
    middle_v,
    last,
    near_place,
    partial,
    incoming,
    edge,
    outbox,
    inbox,
    local_sem,
    send_sem,
    recv_sem,
    value_send,
    value_recv,
):
    channels, span_x, span_y, span_z = geo.shape
    count = place.shape[1]
    peers = bricks * sects
    cap = 5 * count // (4 * peers)
    half = peers // 2 * cap
    brick = lax.axis_index("brick")
    sect = lax.axis_index("sect")
    slab = lax.axis_index("slab")
    column = sect * slabs + slab
    columns = sects * slabs
    me = brick * sects + sect
    linear = me * slabs + slab
    everyone = peers * slabs

    row_order = (0, span_x - 1) + tuple(range(1, span_x - 1))
    row_loads = {
        x: pltpu.make_async_copy(
            geometry.at[:, pl.ds(x, 1)], geo.at[:, pl.ds(x, 1)], local_sem.at[8 + x]
        )
        for x in row_order
    }
    loads = [
        pltpu.make_async_copy(source, landing, local_sem.at[i])
        for i, (source, landing) in enumerate(
            (
                (place_in, place),
                (target_in, target),
                (kernels, taps),
                (attr_in, attr),
                (first, first_v),
                (middle, middle_v),
                (last_in, last),
            )
        )
    ]

    barrier = pltpu.get_barrier_semaphore()
    for j in range(1, everyone):
        other = lax.rem(linear + j, everyone)
        pl.semaphore_signal(
            barrier,
            inc=1,
            device_id={
                "brick": other // columns,
                "sect": other % columns // slabs,
                "slab": other % slabs,
            },
            device_id_type=MESH,
        )

    for x in row_order:
        row_loads[x].start()
    for load in loads:
        load.start()

    def inside(dx, dy):
        b, c = brick + dx, column + dy
        return (b >= 0) & (b < bricks) & (c >= 0) & (c < columns)

    def remote(source, landing, phase, k):
        dx, dy = DIRECTIONS[k]
        c = column + dy
        return pltpu.make_async_remote_copy(
            src_ref=source,
            dst_ref=landing,
            send_sem=send_sem.at[phase, k],
            recv_sem=recv_sem.at[phase, k],
            device_id={"brick": brick + dx, "sect": c // slabs, "slab": c % slabs},
            device_id_type=MESH,
        )

    def halo_copy(phase, k):
        dx, dy = DIRECTIONS[k]
        if phase == 1 and dy == 0:
            return remote(partial.at[k], incoming.at[k], phase, k)
        if phase == 0 and dy == 0:
            row = pl.ds(span_x - 1 if dx == 1 else 0, 1)
            return remote(geometry.at[:, row], edge.at[k], phase, k)
        if phase == 2:
            return remote(place, near_place.at[k], phase, k)
        buffer = (pad, lat)[phase]
        return remote(
            buffer.at[send_range(dx, span_x), send_range(dy, span_y)],
            buffer.at[land_range(dx, span_x), land_range(dy, span_y)],
            phase,
            k,
        )

    def start(phase, which):
        for k in which:
            @pl.when(inside(*DIRECTIONS[k]))
            def _():
                halo_copy(phase, k).start()

    def land(phase, which):
        for k in which:
            dx, dy = DIRECTIONS[k]

            @pl.when(inside(-dx, -dy))
            def _():
                halo_copy(phase, k).wait_recv()

    def drain(phase, which):
        for k in which:
            @pl.when(inside(*DIRECTIONS[k]))
            def _():
                halo_copy(phase, k).wait_send()

    def turn(x, source):
        base = x * channels * span_y
        wide[base:base + channels * span_y] = source.astype(jnp.float32).reshape(
            channels * span_y, span_z
        )
        for y in range(span_y):
            pad[x, y + 1] = wide[pl.ds(base + y, channels, stride=span_y), :].astype(jnp.bfloat16)

    cells = lax.broadcasted_iota(jnp.int32, (span_z, count), 0).astype(jnp.float32) + 0.5

    def weights(points):
        local_x = points[0:1, :] * span_x
        local_y = points[1:2, :] * span_y
        local_z = points[2:3, :] * span_z
        return (
            [hat(local_x - (x - 0.5)) for x in range(span_x + 2)],
            [hat(local_y - (y - 0.5)) for y in range(span_y + 2)],
            hat(local_z - cells).astype(jnp.bfloat16),
        )

    pl.semaphore_wait(barrier, everyone - 1)
    start(0, (0, 1))
    loads[0].wait()
    start(2, (0, 1))
    for x in row_order[:2]:
        row_loads[x].wait()
        turn(x + 1, geo[:, x])
    start(0, range(2, 6))
    for x in row_order[2:]:
        row_loads[x].wait()
        turn(x + 1, geo[:, x])
    start(0, (6, 7))

    own_weights = weights(place)

    loads[1].wait()
    named = lax.broadcasted_iota(jnp.int32, (peers, count), 0)
    onehot = named == target[...]
    earlier = lax.broadcasted_iota(jnp.int32, (count, count), 0) < lax.broadcasted_iota(
        jnp.int32, (count, count), 1
    )
    before = dot(onehot.astype(jnp.bfloat16), earlier.astype(jnp.bfloat16))
    named_brick = lax.div(named, jnp.int32(sects))
    named_sect = named - named_brick * sects
    upper = (named_sect >= sects // 2).astype(jnp.int32)
    block = upper * (peers // 2) + named_brick * (sects // 2) + named_sect - upper * (sects // 2)
    position = jnp.sum(
        jnp.where(onehot, before + (block * cap).astype(jnp.float32), 0.0), axis=0, keepdims=True
    )
    slots = lax.broadcasted_iota(jnp.int32, (2 * half, count), 0)
    gather = (slots == position.astype(jnp.int32)).astype(jnp.bfloat16)

    for k, (dx, dy) in enumerate(DIRECTIONS):
        @pl.when(jnp.logical_not(inside(-dx, -dy)))
        def _():
            if dy != 0:
                for buffer in (pad, lat):
                    region = buffer.at[land_range(dx, span_x), land_range(dy, span_y)]
                    region[...] = jnp.zeros(region.shape, jnp.bfloat16)
            else:
                edge[k] = jnp.zeros(edge.shape[1:], jnp.bfloat16)
                near_place[k] = jnp.zeros(near_place.shape[1:], jnp.float32)
                incoming[k] = jnp.zeros(incoming.shape[1:], jnp.bfloat16)

    loads[2].wait()
    for a in range(3):
        for b in range(3):
            for e in range(3):
                tap = taps[0, a, b, e].astype(jnp.float32).T.astype(jnp.bfloat16)
                low = (a * 3 + b) * channels
                taps_t[e * channels:(e + 1) * channels, low:low + channels] = tap

    lane = lax.broadcasted_iota(jnp.int32, (channels, span_z), 1)

    def product(x, y, low, high):
        near = jnp.concatenate(
            [
                jnp.concatenate(
                    [pad[x + a, y + i:y + i + 3].reshape(3 * channels, span_z) for i in (0, 1)],
                    axis=1,
                )
                for a in range(low, high)
            ],
            axis=0,
        )
        return dot(taps_t[:, low * 3 * channels:high * 3 * channels], near)

    def finish(x, y, pair):
        for i in (0, 1):
            part = pair[:, i * span_z:(i + 1) * span_z]
            left = pltpu.roll(part[:channels], 1, 1)
            right = pltpu.roll(part[2 * channels:], span_z - 1, 1)
            response = (
                part[channels:2 * channels]
                + jnp.where(lane == 0, 0.0, left)
                + jnp.where(lane == span_z - 1, 0.0, right)
            )
            old = pad[x + 1, y + i + 1].astype(jnp.float32)
            lat[x + 1, y + i + 1] = (old + gelu(response)).astype(jnp.bfloat16)

    land(0, (6, 7))
    for x in range(1, span_x - 1):
        for y in range(0, span_y, 2):
            finish(x, y, product(x, y, 0, 3))
    early = [
        [product(x, y, low, high) for y in range(0, span_y, 2)]
        for x, low, high in ((0, 1, 3), (span_x - 1, 0, 2))
    ]
    land(0, range(6))
    turn(0, edge[0, :, 0])
    turn(span_x + 1, edge[1, :, 0])
    for side, (x, a) in enumerate(((0, 0), (span_x - 1, 2))):
        for y in range(0, span_y, 2):
            finish(x, y, early[side][y // 2] + product(x, y, a, a + 1))
    start(1, range(2, 8))

    def sample(of_weights, x, weight, low, high):
        weight_y, weight_z = of_weights[1:]
        part = dot(lat[x, low:high].reshape((high - low) * channels, span_z), weight_z)
        inner = None
        for y in range(low, high):
            term = part[(y - low) * channels:(y - low + 1) * channels] * weight_y[y]
            inner = term if inner is None else inner + term
        return inner * weight

    land(2, (0, 1))
    for k, x, weight in ((0, span_x, 0), (1, 1, span_x + 1)):
        theirs = weights(near_place.at[1 - k])
        partial[k] = sample(theirs, x, theirs[0][weight], 1, span_y + 1).astype(jnp.bfloat16)
    start(1, (0, 1))

    weight_x = own_weights[0]
    total = None
    for x in range(1, span_x + 1):
        term = sample(own_weights, x, weight_x[x], 1, span_y + 1)
        total = term if total is None else total + term
    land(1, range(2, 8))
    for x in range(span_x + 2):
        total = total + sample(own_weights, x, weight_x[x], 0, 1)
        total = total + sample(own_weights, x, weight_x[x], span_y + 1, span_y + 2)
    for load in loads[3:]:
        load.wait()
    land(1, (0, 1))
    total = total + incoming[0].astype(jnp.float32) + incoming[1].astype(jnp.float32)
    row = jnp.concatenate([total.astype(jnp.bfloat16), attr[...]], axis=0)
    table = lax.dot_general(gather, row, NT, preferred_element_type=jnp.float32)
    table = table.astype(jnp.bfloat16)

    acts = [
        gelu(dot(table[s * half:(s + 1) * half], first_v[s])).astype(jnp.bfloat16) for s in range(2)
    ]
    for layer in range(middle_v.shape[1]):
        acts = [gelu(dot(acts[s], middle_v[s, layer])).astype(jnp.bfloat16) for s in range(2)]
    outbox[...] = jnp.zeros(outbox.shape, jnp.float32)
    for s in range(2):
        value = lax.dot_general(last[s], acts[s], NT, preferred_element_type=jnp.float32)
        outbox[s, 0:value.shape[0], 0:half] = value

    def value_copy(j):
        other = lax.rem(me + j, peers)
        there = other % sects
        return pltpu.make_async_remote_copy(
            src_ref=outbox.at[there // (sects // 2)],
            dst_ref=inbox.at[me],
            send_sem=value_send.at[j],
            recv_sem=value_recv.at[j],
            device_id={"brick": other // sects, "sect": there},
            device_id_type=MESH,
        )

    for j in range(1, peers):
        value_copy(j).start()
    inbox[me] = outbox[sect // (sects // 2)]
    drain(0, range(8))
    drain(1, range(8))
    drain(2, (0, 1))
    for j in range(1, peers):
        value_copy(j).wait()

    width = inbox.shape[2]
    own = (brick * (sects // 2) + sect % (sects // 2)) * cap
    rolled = pltpu.roll(inbox[...].reshape(peers * 8, width), lax.rem(width - own, width), 1)
    for i in range(peers):
        out[:, i * cap:(i + 1) * cap] = rolled[i * 8:i * 8 + out.shape[0], 0:cap]


def on_device(
    sizes,
    geometry,
    conv_kernels,
    point_place,
    point_attr,
    destination,
    dense_first,
    dense_middle,
    dense_last,
):
    bricks, sects, slabs = sizes
    channels, span_x, span_y, span_z = geometry.shape
    count = point_place.shape[1]
    peers = bricks * sects
    cap = 5 * count // (4 * peers)
    width = -(-(peers // 2 * cap) // 128) * 128
    padded = (span_x + 2, span_y + 2, channels, span_z)
    attr = point_attr.T
    target = destination.reshape(1, count)
    return pl.pallas_call(
        functools.partial(kernel, bricks, sects, slabs),
        out_shape=pltpu.VMEM((dense_last.shape[1], peers * cap), jnp.float32),
        in_specs=[pl.BlockSpec(memory_space=pl.ANY)] * 8,
        out_specs=pl.BlockSpec(memory_space=pltpu.VMEM),
        scratch_shapes=[
            pltpu.VMEM(geometry.shape, jnp.bfloat16),
            pltpu.VMEM(((span_x + 2) * channels * span_y, span_z), jnp.float32),
            pltpu.VMEM(padded, jnp.bfloat16),
            pltpu.VMEM(padded, jnp.bfloat16),
            pltpu.VMEM(conv_kernels.shape, jnp.bfloat16),
            pltpu.VMEM((3 * channels, 9 * channels), jnp.bfloat16),
            pltpu.VMEM(point_place.shape, jnp.float32),
            pltpu.VMEM(attr.shape, jnp.bfloat16),
            pltpu.VMEM(target.shape, jnp.int32),
            pltpu.VMEM(dense_first.shape, jnp.bfloat16),
            pltpu.VMEM(dense_middle.shape, jnp.bfloat16),
            pltpu.VMEM(dense_last.shape, jnp.bfloat16),
            pltpu.VMEM((2,) + point_place.shape, jnp.float32),
            pltpu.VMEM((2, channels, count), jnp.bfloat16),
            pltpu.VMEM((2, channels, count), jnp.bfloat16),
            pltpu.VMEM((2, channels, 1, span_y, span_z), jnp.bfloat16),
            pltpu.VMEM((2, 8, width), jnp.float32),
            pltpu.VMEM((peers, 8, width), jnp.float32),
            pltpu.SemaphoreType.DMA((8 + span_x,)),
            pltpu.SemaphoreType.DMA((3, 8)),
            pltpu.SemaphoreType.DMA((3, 8)),
            pltpu.SemaphoreType.DMA((peers,)),
            pltpu.SemaphoreType.DMA((peers,)),
        ],
        compiler_params=pltpu.CompilerParams(
            collective_id=0, has_side_effects=True, vmem_limit_bytes=60 * 2**20
        ),
    )(
        geometry,
        conv_kernels,
        point_place,
        attr,
        target,
        dense_first,
        dense_middle,
        dense_last,
    )


def solution(mesh):
    sizes = tuple(mesh.shape[axis] for axis in ("brick", "sect", "slab"))
    in_specs = (
        P(None, ("case", "brick"), ("sect", "slab"), None),
        P(),
        P(None, ("case", "brick", "sect", "slab")),
        P(("case", "brick", "sect", "slab"), None),
        P(("case", "brick", "sect", "slab"), None),
        P(),
        P(),
        P(),
    )
    out_specs = P(None, ("case", "brick", "sect", "slab"))
    return jax.shard_map(
        functools.partial(on_device, sizes),
        mesh=mesh,
        in_specs=in_specs,
        out_specs=out_specs,
        check_vma=False,
    )
```

```python
import functools
import math

import jax
import jax.numpy as jnp
from jax import lax
from jax.experimental import pallas as pl
from jax.experimental.pallas import tpu as pltpu
from jax.sharding import PartitionSpec as P

MESH = pl.DeviceIdType.MESH
DIRECTIONS = ((1, 0), (-1, 0), (1, 1), (1, -1), (-1, 1), (-1, -1), (0, 1), (0, -1))
NT = (((1,), (1,)), ((), ()))


def hat(offset):
    return jnp.maximum(0.0, 1.0 - jnp.abs(offset))


def gelu(value):
    scale = (2.0 / math.pi) ** 0.5
    middle = 0.5 * value
    return middle + middle * jnp.tanh(value * (scale + (scale * 0.044715) * (value * value)))


def dot(a, b):
    return jnp.dot(a, b, preferred_element_type=jnp.float32)


def send_range(step, size):
    return {1: pl.ds(size, 1), -1: pl.ds(1, 1), 0: pl.ds(1, size)}[step]


def land_range(step, size):
    return {1: pl.ds(0, 1), -1: pl.ds(size + 1, 1), 0: pl.ds(1, size)}[step]


def kernel(
    bricks,
    sects,
    slabs,
    geometry,
    kernels,
    place_in,
    attr_in,
    target_in,
    first,
    middle,
    last_in,
    out,
    geo,
    wide,
    pad,
    lat,
    taps,
    taps_t,
    place,
    attr,
    target,
    first_v,
    middle_v,
    last,
    near_place,
    partial,
    incoming,
    edge,
    outbox,
    inbox,
    local_sem,
    send_sem,
    recv_sem,
    value_send,
    value_recv,
):
    channels, span_x, span_y, span_z = geo.shape
    count = place.shape[1]
    peers = bricks * sects
    cap = 5 * count // (4 * peers)
    half = peers // 2 * cap
    brick = lax.axis_index("brick")
    sect = lax.axis_index("sect")
    slab = lax.axis_index("slab")
    column = sect * slabs + slab
    columns = sects * slabs
    me = brick * sects + sect
    linear = me * slabs + slab
    everyone = peers * slabs

    row_order = (0, span_x - 1) + tuple(range(1, span_x - 1))
    row_loads = {
        x: pltpu.make_async_copy(
            geometry.at[:, pl.ds(x, 1)], geo.at[:, pl.ds(x, 1)], local_sem.at[8 + x]
        )
        for x in row_order
    }
    loads = [
        pltpu.make_async_copy(source, landing, local_sem.at[i])
        for i, (source, landing) in enumerate(
            (
                (place_in, place),
                (target_in, target),
                (kernels, taps),
                (attr_in, attr),
                (first, first_v),
                (middle, middle_v),
                (last_in, last),
            )
        )
    ]

    barrier = pltpu.get_barrier_semaphore()
    for j in range(1, everyone):
        other = lax.rem(linear + j, everyone)
        pl.semaphore_signal(
            barrier,
            inc=1,
            device_id={
                "brick": lax.div(other, columns),
                "sect": lax.div(lax.rem(other, columns), slabs),
                "slab": lax.rem(other, slabs),
            },
            device_id_type=MESH,
        )

    for x in row_order:
        row_loads[x].start()
    for load in loads:
        load.start()

    def inside(dx, dy):
        b, c = brick + dx, column + dy
        return (b >= 0) & (b < bricks) & (c >= 0) & (c < columns)

    def remote(source, landing, phase, k):
        dx, dy = DIRECTIONS[k]
        c = column + dy
        return pltpu.make_async_remote_copy(
            src_ref=source,
            dst_ref=landing,
            send_sem=send_sem.at[phase, k],
            recv_sem=recv_sem.at[phase, k],
            device_id={"brick": brick + dx, "sect": lax.div(c, slabs), "slab": lax.rem(c, slabs)},
            device_id_type=MESH,
        )

    def halo_copy(phase, k):
        dx, dy = DIRECTIONS[k]
        if phase == 1 and dy == 0:
            return remote(partial.at[k], incoming.at[k], phase, k)
        if phase == 0 and dy == 0:
            row = pl.ds(span_x - 1 if dx == 1 else 0, 1)
            return remote(geometry.at[:, row], edge.at[k], phase, k)
        if phase == 2:
            return remote(place, near_place.at[k], phase, k)
        buffer = (pad, lat)[phase]
        return remote(
            buffer.at[send_range(dx, span_x), send_range(dy, span_y)],
            buffer.at[land_range(dx, span_x), land_range(dy, span_y)],
            phase,
            k,
        )

    def start(phase, which):
        for k in which:
            @pl.when(inside(*DIRECTIONS[k]))
            def _():
                halo_copy(phase, k).start()

    def land(phase, which):
        for k in which:
            dx, dy = DIRECTIONS[k]

            @pl.when(inside(-dx, -dy))
            def _():
                halo_copy(phase, k).wait_recv()

    def drain(phase, which):
        for k in which:
            @pl.when(inside(*DIRECTIONS[k]))
            def _():
                halo_copy(phase, k).wait_send()

    def turn(x, source):
        base = x * channels * span_y
        wide[base:base + channels * span_y] = source.astype(jnp.float32).reshape(
            channels * span_y, span_z
        )
        for y in range(span_y):
            pad[x, y + 1] = wide[pl.ds(base + y, channels, stride=span_y), :].astype(jnp.bfloat16)

    cells = lax.broadcasted_iota(jnp.int32, (span_z, count), 0).astype(jnp.float32) + 0.5

    def weights(points):
        local_x = points[0:1, :] * span_x
        local_y = points[1:2, :] * span_y
        local_z = points[2:3, :] * span_z
        return (
            [hat(local_x - (x - 0.5)) for x in range(span_x + 2)],
            [hat(local_y - (y - 0.5)) for y in range(span_y + 2)],
            hat(local_z - cells).astype(jnp.bfloat16),
        )

    pl.semaphore_wait(barrier, everyone - 1)
    start(0, (0, 1))
    loads[0].wait()
    start(2, (0, 1))
    for x in row_order[:2]:
        row_loads[x].wait()
        turn(x + 1, geo[:, x])
    start(0, range(2, 6))
    for x in row_order[2:]:
        row_loads[x].wait()
        turn(x + 1, geo[:, x])
    start(0, (6, 7))

    for k, (dx, dy) in enumerate(DIRECTIONS):
        @pl.when(jnp.logical_not(inside(-dx, -dy)))
        def _():
            if dy != 0:
                for buffer in (pad, lat):
                    region = buffer.at[land_range(dx, span_x), land_range(dy, span_y)]
                    region[...] = jnp.zeros(region.shape, jnp.bfloat16)
            else:
                edge[k] = jnp.zeros(edge.shape[1:], jnp.bfloat16)
                near_place[k] = jnp.zeros(near_place.shape[1:], jnp.float32)
                incoming[k] = jnp.zeros(incoming.shape[1:], jnp.bfloat16)

    loads[2].wait()
    for a in range(3):
        for b in range(3):
            for e in range(3):
                tap = taps[0, a, b, e].astype(jnp.float32).T.astype(jnp.bfloat16)
                low = (a * 3 + b) * channels
                taps_t[e * channels:(e + 1) * channels, low:low + channels] = tap

    lane = lax.broadcasted_iota(jnp.int32, (channels, span_z), 1)

    def product(x, y, low, high):
        near = jnp.concatenate(
            [
                jnp.concatenate(
                    [pad[x + a, y + i:y + i + 3].reshape(3 * channels, span_z) for i in (0, 1)],
                    axis=1,
                )
                for a in range(low, high)
            ],
            axis=0,
        )
        return dot(taps_t[:, low * 3 * channels:high * 3 * channels], near)

    def finish(x, y, pair):
        for i in (0, 1):
            part = pair[:, i * span_z:(i + 1) * span_z]
            left = pltpu.roll(part[:channels], 1, 1)
            right = pltpu.roll(part[2 * channels:], span_z - 1, 1)
            response = (
                part[channels:2 * channels]
                + jnp.where(lane == 0, 0.0, left)
                + jnp.where(lane == span_z - 1, 0.0, right)
            )
            old = pad[x + 1, y + i + 1].astype(jnp.float32)
            lat[x + 1, y + i + 1] = (old + gelu(response)).astype(jnp.bfloat16)

    land(0, (6, 7))
    for x in range(1, span_x - 1):
        for y in range(0, span_y, 2):
            finish(x, y, product(x, y, 0, 3))
    early = [
        [product(x, y, low, high) for y in range(0, span_y, 2)]
        for x, low, high in ((0, 1, 3), (span_x - 1, 0, 2))
    ]
    land(2, (0, 1))
    theirs = [weights(near_place.at[1 - k]) for k in (0, 1)]
    land(0, range(6))
    turn(0, edge[0, :, 0])
    turn(span_x + 1, edge[1, :, 0])
    for side, (x, a) in enumerate(((0, 0), (span_x - 1, 2))):
        for y in range(0, span_y, 2):
            finish(x, y, early[side][y // 2] + product(x, y, a, a + 1))
    start(1, range(2, 8))

    def sample(of_weights, x, weight, low, high):
        weight_y, weight_z = of_weights[1:]
        part = dot(lat[x, low:high].reshape((high - low) * channels, span_z), weight_z)
        inner = None
        for y in range(low, high):
            term = part[(y - low) * channels:(y - low + 1) * channels] * weight_y[y]
            inner = term if inner is None else inner + term
        return inner * weight

    for k, x, weight in ((0, span_x, 0), (1, 1, span_x + 1)):
        weight_x = theirs[k][0][weight]
        partial[k] = sample(theirs[k], x, weight_x, 1, span_y + 1).astype(jnp.bfloat16)
        start(1, (k,))

    own_weights = weights(place)

    loads[1].wait()
    named = lax.broadcasted_iota(jnp.int32, (peers, count), 0)
    onehot = named == target[...]
    earlier = lax.broadcasted_iota(jnp.int32, (count, count), 0) < lax.broadcasted_iota(
        jnp.int32, (count, count), 1
    )
    before = dot(onehot.astype(jnp.bfloat16), earlier.astype(jnp.bfloat16))
    named_brick = lax.div(named, jnp.int32(sects))
    named_sect = named - named_brick * sects
    upper = (named_sect >= sects // 2).astype(jnp.int32)
    block = upper * (peers // 2) + named_brick * (sects // 2) + named_sect - upper * (sects // 2)
    position = jnp.sum(
        jnp.where(onehot, before + (block * cap).astype(jnp.float32), 0.0), axis=0, keepdims=True
    )
    slots = lax.broadcasted_iota(jnp.int32, (2 * half, count), 0)
    gather = (slots == position.astype(jnp.int32)).astype(jnp.bfloat16)


    outbox[...] = jnp.zeros(outbox.shape, jnp.float32)
    weight_x, weight_y, weight_z = own_weights
    total = None
    for x in range(1, span_x + 1):
        term = sample(own_weights, x, weight_x[x], 1, span_y + 1)
        total = term if total is None else total + term
    land(1, range(2, 8))
    for y in (0, span_y + 1):
        part = dot(lat[:, y].reshape((span_x + 2) * channels, span_z), weight_z)
        inner = part[:channels] * weight_x[0]
        for x in range(1, span_x + 2):
            inner = inner + part[x * channels:(x + 1) * channels] * weight_x[x]
        total = total + inner * weight_y[y]
    for load in loads[3:]:
        load.wait()
    land(1, (0, 1))
    total = total + incoming[0].astype(jnp.float32) + incoming[1].astype(jnp.float32)
    row = jnp.concatenate([total.astype(jnp.bfloat16), attr[...]], axis=0)
    table = lax.dot_general(gather, row, NT, preferred_element_type=jnp.float32)
    table = table.astype(jnp.bfloat16)

    acts = [
        gelu(dot(table[s * half:(s + 1) * half], first_v[s])).astype(jnp.bfloat16) for s in range(2)
    ]
    for layer in range(middle_v.shape[1]):
        acts = [gelu(dot(acts[s], middle_v[s, layer])).astype(jnp.bfloat16) for s in range(2)]
    for s in range(2):
        value = lax.dot_general(last[s], acts[s], NT, preferred_element_type=jnp.float32)
        outbox[s, 0:value.shape[0], 0:half] = value

    def value_copy(j):
        other = lax.rem(me + j, peers)
        there = lax.rem(other, sects)
        return pltpu.make_async_remote_copy(
            src_ref=outbox.at[lax.div(there, sects // 2)],
            dst_ref=inbox.at[me],
            send_sem=value_send.at[j],
            recv_sem=value_recv.at[j],
            device_id={"brick": lax.div(other, sects), "sect": there},
            device_id_type=MESH,
        )

    for j in range(1, peers):
        value_copy(j).start()
    inbox[me] = outbox[lax.div(sect, sects // 2)]
    drain(0, range(8))
    drain(1, range(8))
    drain(2, (0, 1))
    for j in range(1, peers):
        value_copy(j).wait()

    width = inbox.shape[2]
    own = (brick * (sects // 2) + sect % (sects // 2)) * cap
    rolled = pltpu.roll(inbox[...].reshape(peers * 8, width), lax.rem(width - own, width), 1)
    for i in range(peers):
        out[:, i * cap:(i + 1) * cap] = rolled[i * 8:i * 8 + out.shape[0], 0:cap]


def on_device(
    sizes,
    geometry,
    conv_kernels,
    point_place,
    point_attr,
    destination,
    dense_first,
    dense_middle,
    dense_last,
):
    bricks, sects, slabs = sizes
    channels, span_x, span_y, span_z = geometry.shape
    count = point_place.shape[1]
    peers = bricks * sects
    cap = 5 * count // (4 * peers)
    width = -(-(peers // 2 * cap) // 128) * 128
    padded = (span_x + 2, span_y + 2, channels, span_z)
    attr = point_attr.T
    target = destination.reshape(1, count)
    return pl.pallas_call(
        functools.partial(kernel, bricks, sects, slabs),
        out_shape=pltpu.VMEM((dense_last.shape[1], peers * cap), jnp.float32),
        in_specs=[pl.BlockSpec(memory_space=pl.ANY)] * 8,
        out_specs=pl.BlockSpec(memory_space=pltpu.VMEM),
        scratch_shapes=[
            pltpu.VMEM(geometry.shape, jnp.bfloat16),
            pltpu.VMEM(((span_x + 2) * channels * span_y, span_z), jnp.float32),
            pltpu.VMEM(padded, jnp.bfloat16),
            pltpu.VMEM(padded, jnp.bfloat16),
            pltpu.VMEM(conv_kernels.shape, jnp.bfloat16),
            pltpu.VMEM((3 * channels, 9 * channels), jnp.bfloat16),
            pltpu.VMEM(point_place.shape, jnp.float32),
            pltpu.VMEM(attr.shape, jnp.bfloat16),
            pltpu.VMEM(target.shape, jnp.int32),
            pltpu.VMEM(dense_first.shape, jnp.bfloat16),
            pltpu.VMEM(dense_middle.shape, jnp.bfloat16),
            pltpu.VMEM(dense_last.shape, jnp.bfloat16),
            pltpu.VMEM((2,) + point_place.shape, jnp.float32),
            pltpu.VMEM((2, channels, count), jnp.bfloat16),
            pltpu.VMEM((2, channels, count), jnp.bfloat16),
            pltpu.VMEM((2, channels, 1, span_y, span_z), jnp.bfloat16),
            pltpu.VMEM((2, 8, width), jnp.float32),
            pltpu.VMEM((peers, 8, width), jnp.float32),
            pltpu.SemaphoreType.DMA((8 + span_x,)),
            pltpu.SemaphoreType.DMA((3, 8)),
            pltpu.SemaphoreType.DMA((3, 8)),
            pltpu.SemaphoreType.DMA((peers,)),
            pltpu.SemaphoreType.DMA((peers,)),
        ],
        compiler_params=pltpu.CompilerParams(
            collective_id=0, has_side_effects=True, vmem_limit_bytes=60 * 2**20
        ),
    )(
        geometry,
        conv_kernels,
        point_place,
        attr,
        target,
        dense_first,
        dense_middle,
        dense_last,
    )


def solution(mesh):
    sizes = tuple(mesh.shape[axis] for axis in ("brick", "sect", "slab"))
    in_specs = (
        P(None, ("case", "brick"), ("sect", "slab"), None),
        P(),
        P(None, ("case", "brick", "sect", "slab")),
        P(("case", "brick", "sect", "slab"), None),
        P(("case", "brick", "sect", "slab"), None),
        P(),
        P(),
        P(),
    )
    out_specs = P(None, ("case", "brick", "sect", "slab"))
    return jax.shard_map(
        functools.partial(on_device, sizes),
        mesh=mesh,
        in_specs=in_specs,
        out_specs=out_specs,
        check_vma=False,
    )
```

```python
import functools
import math

import jax
import jax.numpy as jnp
from jax import lax
from jax.experimental import pallas as pl
from jax.experimental.pallas import tpu as pltpu
from jax.sharding import PartitionSpec as P

MESH = pl.DeviceIdType.MESH
DIRECTIONS = ((1, 0), (-1, 0), (1, 1), (1, -1), (-1, 1), (-1, -1), (0, 1), (0, -1))
NT = (((1,), (1,)), ((), ()))


def hat(offset):
    return jnp.maximum(0.0, 1.0 - jnp.abs(offset))


def gelu(value):
    scale = (2.0 / math.pi) ** 0.5
    middle = 0.5 * value
    return middle + middle * jnp.tanh(value * (scale + (scale * 0.044715) * (value * value)))


def dot(a, b):
    return jnp.dot(a, b, preferred_element_type=jnp.float32)


def send_range(step, size):
    return {1: pl.ds(size, 1), -1: pl.ds(1, 1), 0: pl.ds(1, size)}[step]


def land_range(step, size):
    return {1: pl.ds(0, 1), -1: pl.ds(size + 1, 1), 0: pl.ds(1, size)}[step]


def kernel(
    bricks,
    sects,
    slabs,
    geometry,
    kernels,
    place_in,
    attr_in,
    target_in,
    first,
    middle,
    last_in,
    out,
    geo,
    wide,
    pad,
    lat,
    taps,
    taps_t,
    place,
    attr,
    target,
    first_v,
    middle_v,
    last,
    near_place,
    partial,
    incoming,
    edge,
    outbox,
    inbox,
    local_sem,
    send_sem,
    recv_sem,
    value_send,
    value_recv,
):
    channels, span_x, span_y, span_z = geo.shape
    count = place.shape[1]
    peers = bricks * sects
    cap = 5 * count // (4 * peers)
    half = peers // 2 * cap
    brick = lax.axis_index("brick")
    sect = lax.axis_index("sect")
    slab = lax.axis_index("slab")
    column = sect * slabs + slab
    columns = sects * slabs
    me = brick * sects + sect
    linear = me * slabs + slab
    everyone = peers * slabs

    row_order = (0, span_x - 1) + tuple(range(1, span_x - 1))
    row_loads = {
        x: pltpu.make_async_copy(
            geometry.at[:, pl.ds(x, 1)], geo.at[:, pl.ds(x, 1)], local_sem.at[8 + x]
        )
        for x in row_order
    }
    loads = [
        pltpu.make_async_copy(source, landing, local_sem.at[i])
        for i, (source, landing) in enumerate(
            (
                (place_in, place),
                (target_in, target),
                (kernels, taps),
                (attr_in, attr),
                (first, first_v),
                (middle, middle_v),
                (last_in, last),
            )
        )
    ]

    def inside(dx, dy):
        b, c = brick + dx, column + dy
        return (b >= 0) & (b < bricks) & (c >= 0) & (c < columns)

    near_only = bricks <= 4 and columns <= 4
    barrier = pltpu.get_barrier_semaphore()
    if near_only:
        for dx, dy in DIRECTIONS:
            @pl.when(inside(dx, dy))
            def _():
                pl.semaphore_signal(
                    barrier,
                    inc=1,
                    device_id={
                        "brick": brick + dx,
                        "sect": lax.div(column + dy, slabs),
                        "slab": lax.rem(column + dy, slabs),
                    },
                    device_id_type=MESH,
                )
        spread_x = 1 + (brick > 0).astype(jnp.int32) + (brick < bricks - 1).astype(jnp.int32)
        spread_y = 1 + (column > 0).astype(jnp.int32) + (column < columns - 1).astype(jnp.int32)
        expected = spread_x * spread_y - 1
    else:
        expected = everyone - 1
        for j in range(1, everyone):
            other = lax.rem(linear + j, everyone)
            pl.semaphore_signal(
                barrier,
                inc=1,
                device_id={
                    "brick": lax.div(other, columns),
                    "sect": lax.div(lax.rem(other, columns), slabs),
                    "slab": lax.rem(other, slabs),
                },
                device_id_type=MESH,
            )

    for x in row_order:
        row_loads[x].start()
    for load in loads:
        load.start()

    def remote(source, landing, phase, k):
        dx, dy = DIRECTIONS[k]
        c = column + dy
        return pltpu.make_async_remote_copy(
            src_ref=source,
            dst_ref=landing,
            send_sem=send_sem.at[phase, k],
            recv_sem=recv_sem.at[phase, k],
            device_id={"brick": brick + dx, "sect": lax.div(c, slabs), "slab": lax.rem(c, slabs)},
            device_id_type=MESH,
        )

    def halo_copy(phase, k):
        dx, dy = DIRECTIONS[k]
        if phase == 1 and dy == 0:
            return remote(partial.at[k], incoming.at[k], phase, k)
        if phase == 0 and dy == 0:
            row = pl.ds(span_x - 1 if dx == 1 else 0, 1)
            return remote(geometry.at[:, row], edge.at[k], phase, k)
        if phase == 2:
            return remote(place, near_place.at[k], phase, k)
        buffer = (pad, lat)[phase]
        return remote(
            buffer.at[send_range(dx, span_x), send_range(dy, span_y)],
            buffer.at[land_range(dx, span_x), land_range(dy, span_y)],
            phase,
            k,
        )

    def start(phase, which):
        for k in which:
            @pl.when(inside(*DIRECTIONS[k]))
            def _():
                halo_copy(phase, k).start()

    def land(phase, which):
        for k in which:
            dx, dy = DIRECTIONS[k]

            @pl.when(inside(-dx, -dy))
            def _():
                halo_copy(phase, k).wait_recv()

    def drain(phase, which):
        for k in which:
            @pl.when(inside(*DIRECTIONS[k]))
            def _():
                halo_copy(phase, k).wait_send()

    def turn(x, source):
        base = x * channels * span_y
        wide[base:base + channels * span_y] = source.astype(jnp.float32).reshape(
            channels * span_y, span_z
        )
        for y in range(span_y):
            pad[x, y + 1] = wide[pl.ds(base + y, channels, stride=span_y), :].astype(jnp.bfloat16)

    cells = lax.broadcasted_iota(jnp.int32, (span_z, count), 0).astype(jnp.float32) + 0.5

    def weights(points):
        local_x = points[0:1, :] * span_x
        local_y = points[1:2, :] * span_y
        local_z = points[2:3, :] * span_z
        return (
            [hat(local_x - (x - 0.5)) for x in range(span_x + 2)],
            [hat(local_y - (y - 0.5)) for y in range(span_y + 2)],
            hat(local_z - cells).astype(jnp.bfloat16),
        )

    pl.semaphore_wait(barrier, expected)
    start(0, (0, 1))
    loads[0].wait()
    start(2, (0, 1))
    for x in row_order[:2]:
        row_loads[x].wait()
        turn(x + 1, geo[:, x])
    start(0, range(2, 6))
    for x in row_order[2:]:
        row_loads[x].wait()
        turn(x + 1, geo[:, x])
    start(0, (6, 7))

    for k, (dx, dy) in enumerate(DIRECTIONS):
        @pl.when(jnp.logical_not(inside(-dx, -dy)))
        def _():
            if dy != 0:
                for buffer in (pad, lat):
                    region = buffer.at[land_range(dx, span_x), land_range(dy, span_y)]
                    region[...] = jnp.zeros(region.shape, jnp.bfloat16)
            else:
                edge[k] = jnp.zeros(edge.shape[1:], jnp.bfloat16)
                near_place[k] = jnp.zeros(near_place.shape[1:], jnp.float32)
                incoming[k] = jnp.zeros(incoming.shape[1:], jnp.bfloat16)

    loads[2].wait()
    for a in range(3):
        for b in range(3):
            for e in range(3):
                tap = taps[0, a, b, e].astype(jnp.float32).T.astype(jnp.bfloat16)
                low = (a * 3 + b) * channels
                taps_t[e * channels:(e + 1) * channels, low:low + channels] = tap

    lane = lax.broadcasted_iota(jnp.int32, (channels, span_z), 1)

    def product(x, y, low, high):
        near = jnp.concatenate(
            [
                jnp.concatenate(
                    [pad[x + a, y + i:y + i + 3].reshape(3 * channels, span_z) for i in (0, 1)],
                    axis=1,
                )
                for a in range(low, high)
            ],
            axis=0,
        )
        return dot(taps_t[:, low * 3 * channels:high * 3 * channels], near)

    def finish(x, y, pair):
        for i in (0, 1):
            part = pair[:, i * span_z:(i + 1) * span_z]
            left = pltpu.roll(part[:channels], 1, 1)
            right = pltpu.roll(part[2 * channels:], span_z - 1, 1)
            response = (
                part[channels:2 * channels]
                + jnp.where(lane == 0, 0.0, left)
                + jnp.where(lane == span_z - 1, 0.0, right)
            )
            old = pad[x + 1, y + i + 1].astype(jnp.float32)
            lat[x + 1, y + i + 1] = (old + gelu(response)).astype(jnp.bfloat16)

    early = {}

    def inner_rows(some):
        for x in range(1, span_x - 1):
            for y in some:
                finish(x, y, product(x, y, 0, 3))
        for x, low, high in ((0, 1, 3), (span_x - 1, 0, 2)):
            for y in some:
                early[x, y] = product(x, y, low, high)

    inner_rows(range(2, span_y - 2, 2))
    land(0, (6, 7))
    inner_rows((0, span_y - 2))
    land(2, (0, 1))
    theirs = [weights(near_place.at[1 - k]) for k in (0, 1)]
    land(0, range(6))
    turn(0, edge[0, :, 0])
    turn(span_x + 1, edge[1, :, 0])
    for x, a in ((0, 0), (span_x - 1, 2)):
        for y in range(0, span_y, 2):
            finish(x, y, early[x, y] + product(x, y, a, a + 1))
    start(1, range(2, 8))

    def sample(of_weights, x, weight, low, high):
        weight_y, weight_z = of_weights[1:]
        part = dot(lat[x, low:high].reshape((high - low) * channels, span_z), weight_z)
        inner = None
        for y in range(low, high):
            term = part[(y - low) * channels:(y - low + 1) * channels] * weight_y[y]
            inner = term if inner is None else inner + term
        return inner * weight

    for k, x, weight in ((0, span_x, 0), (1, 1, span_x + 1)):
        weight_x = theirs[k][0][weight]
        partial[k] = sample(theirs[k], x, weight_x, 1, span_y + 1).astype(jnp.bfloat16)
        start(1, (k,))

    own_weights = weights(place)

    loads[1].wait()
    named = lax.broadcasted_iota(jnp.int32, (peers, count), 0)
    onehot = named == target[...]
    earlier = lax.broadcasted_iota(jnp.int32, (count, count), 0) < lax.broadcasted_iota(
        jnp.int32, (count, count), 1
    )
    before = dot(onehot.astype(jnp.bfloat16), earlier.astype(jnp.bfloat16))
    named_brick = lax.div(named, jnp.int32(sects))
    named_sect = named - named_brick * sects
    upper = (named_sect >= sects // 2).astype(jnp.int32)
    block = upper * (peers // 2) + named_brick * (sects // 2) + named_sect - upper * (sects // 2)
    position = jnp.sum(
        jnp.where(onehot, before + (block * cap).astype(jnp.float32), 0.0), axis=0, keepdims=True
    )
    slots = lax.broadcasted_iota(jnp.int32, (2 * half, count), 0)
    gather = (slots == position.astype(jnp.int32)).astype(jnp.bfloat16)


    outbox[...] = jnp.zeros(outbox.shape, jnp.float32)
    weight_x, weight_y, weight_z = own_weights
    total = None
    for x in range(1, span_x + 1):
        term = sample(own_weights, x, weight_x[x], 1, span_y + 1)
        total = term if total is None else total + term
    land(1, range(2, 8))
    for y in (0, span_y + 1):
        part = dot(lat[:, y].reshape((span_x + 2) * channels, span_z), weight_z)
        inner = part[:channels] * weight_x[0]
        for x in range(1, span_x + 2):
            inner = inner + part[x * channels:(x + 1) * channels] * weight_x[x]
        total = total + inner * weight_y[y]
    for load in loads[3:]:
        load.wait()
    land(1, (0, 1))
    total = total + incoming[0].astype(jnp.float32) + incoming[1].astype(jnp.float32)
    row = jnp.concatenate([total.astype(jnp.bfloat16), attr[...]], axis=0)
    table = lax.dot_general(gather, row, NT, preferred_element_type=jnp.float32)
    table = table.astype(jnp.bfloat16)

    acts = [
        gelu(dot(table[s * half:(s + 1) * half], first_v[s])).astype(jnp.bfloat16) for s in range(2)
    ]
    for layer in range(middle_v.shape[1]):
        acts = [gelu(dot(acts[s], middle_v[s, layer])).astype(jnp.bfloat16) for s in range(2)]
    for s in range(2):
        value = lax.dot_general(last[s], acts[s], NT, preferred_element_type=jnp.float32)
        outbox[s, 0:value.shape[0], 0:half] = value

    def value_copy(j):
        other = lax.rem(me + j, peers)
        there = lax.rem(other, sects)
        return pltpu.make_async_remote_copy(
            src_ref=outbox.at[lax.div(there, sects // 2)],
            dst_ref=inbox.at[me],
            send_sem=value_send.at[j],
            recv_sem=value_recv.at[j],
            device_id={"brick": lax.div(other, sects), "sect": there},
            device_id_type=MESH,
        )

    for j in range(1, peers):
        value_copy(j).start()
    inbox[me] = outbox[lax.div(sect, sects // 2)]
    drain(0, range(8))
    drain(1, range(8))
    drain(2, (0, 1))
    for j in range(1, peers):
        value_copy(j).wait()

    width = inbox.shape[2]
    own = (brick * (sects // 2) + sect % (sects // 2)) * cap
    rolled = pltpu.roll(inbox[...].reshape(peers * 8, width), lax.rem(width - own, width), 1)
    for i in range(peers):
        out[:, i * cap:(i + 1) * cap] = rolled[i * 8:i * 8 + out.shape[0], 0:cap]


def on_device(
    sizes,
    geometry,
    conv_kernels,
    point_place,
    point_attr,
    destination,
    dense_first,
    dense_middle,
    dense_last,
):
    bricks, sects, slabs = sizes
    channels, span_x, span_y, span_z = geometry.shape
    count = point_place.shape[1]
    peers = bricks * sects
    cap = 5 * count // (4 * peers)
    width = -(-(peers // 2 * cap) // 128) * 128
    padded = (span_x + 2, span_y + 2, channels, span_z)
    attr = point_attr.T
    target = destination.reshape(1, count)
    return pl.pallas_call(
        functools.partial(kernel, bricks, sects, slabs),
        out_shape=pltpu.VMEM((dense_last.shape[1], peers * cap), jnp.float32),
        in_specs=[pl.BlockSpec(memory_space=pl.ANY)] * 8,
        out_specs=pl.BlockSpec(memory_space=pltpu.VMEM),
        scratch_shapes=[
            pltpu.VMEM(geometry.shape, jnp.bfloat16),
            pltpu.VMEM(((span_x + 2) * channels * span_y, span_z), jnp.float32),
            pltpu.VMEM(padded, jnp.bfloat16),
            pltpu.VMEM(padded, jnp.bfloat16),
            pltpu.VMEM(conv_kernels.shape, jnp.bfloat16),
            pltpu.VMEM((3 * channels, 9 * channels), jnp.bfloat16),
            pltpu.VMEM(point_place.shape, jnp.float32),
            pltpu.VMEM(attr.shape, jnp.bfloat16),
            pltpu.VMEM(target.shape, jnp.int32),
            pltpu.VMEM(dense_first.shape, jnp.bfloat16),
            pltpu.VMEM(dense_middle.shape, jnp.bfloat16),
            pltpu.VMEM(dense_last.shape, jnp.bfloat16),
            pltpu.VMEM((2,) + point_place.shape, jnp.float32),
            pltpu.VMEM((2, channels, count), jnp.bfloat16),
            pltpu.VMEM((2, channels, count), jnp.bfloat16),
            pltpu.VMEM((2, channels, 1, span_y, span_z), jnp.bfloat16),
            pltpu.VMEM((2, 8, width), jnp.float32),
            pltpu.VMEM((peers, 8, width), jnp.float32),
            pltpu.SemaphoreType.DMA((8 + span_x,)),
            pltpu.SemaphoreType.DMA((3, 8)),
            pltpu.SemaphoreType.DMA((3, 8)),
            pltpu.SemaphoreType.DMA((peers,)),
            pltpu.SemaphoreType.DMA((peers,)),
        ],
        compiler_params=pltpu.CompilerParams(
            collective_id=0, has_side_effects=True, vmem_limit_bytes=60 * 2**20
        ),
    )(
        geometry,
        conv_kernels,
        point_place,
        attr,
        target,
        dense_first,
        dense_middle,
        dense_last,
    )


def solution(mesh):
    sizes = tuple(mesh.shape[axis] for axis in ("brick", "sect", "slab"))
    in_specs = (
        P(None, ("case", "brick"), ("sect", "slab"), None),
        P(),
        P(None, ("case", "brick", "sect", "slab")),
        P(("case", "brick", "sect", "slab"), None),
        P(("case", "brick", "sect", "slab"), None),
        P(),
        P(),
        P(),
    )
    out_specs = P(None, ("case", "brick", "sect", "slab"))
    return jax.shard_map(
        functools.partial(on_device, sizes),
        mesh=mesh,
        in_specs=in_specs,
        out_specs=out_specs,
        check_vma=False,
    )
```

```python
import functools
import math

import jax
import jax.numpy as jnp
from jax import lax
from jax.experimental import pallas as pl
from jax.experimental.pallas import tpu as pltpu
from jax.sharding import PartitionSpec as P

MESH = pl.DeviceIdType.MESH
DIRECTIONS = ((1, 0), (-1, 0), (1, 1), (1, -1), (-1, 1), (-1, -1), (0, 1), (0, -1))
NT = (((1,), (1,)), ((), ()))


def hat(offset):
    return jnp.maximum(0.0, 1.0 - jnp.abs(offset))


def gelu(value):
    scale = (2.0 / math.pi) ** 0.5
    middle = 0.5 * value
    return middle + middle * jnp.tanh(value * (scale + (scale * 0.044715) * (value * value)))


def dot(a, b):
    return jnp.dot(a, b, preferred_element_type=jnp.float32)


def send_range(step, size):
    return {1: pl.ds(size, 1), -1: pl.ds(1, 1), 0: pl.ds(1, size)}[step]


def land_range(step, size):
    return {1: pl.ds(0, 1), -1: pl.ds(size + 1, 1), 0: pl.ds(1, size)}[step]


def kernel(
    bricks,
    sects,
    slabs,
    geometry,
    kernels,
    place_in,
    attr_in,
    target_in,
    first,
    middle,
    last_in,
    out,
    geo,
    wide,
    pad,
    lat,
    taps,
    taps_t,
    place,
    attr,
    target,
    first_v,
    middle_v,
    last,
    near_place,
    partial,
    incoming,
    edge,
    outbox,
    inbox,
    local_sem,
    send_sem,
    recv_sem,
    value_send,
    value_recv,
):
    channels, span_x, span_y, span_z = geo.shape
    count = place.shape[1]
    peers = bricks * sects
    cap = 5 * count // (4 * peers)
    half = peers // 2 * cap
    brick = lax.axis_index("brick")
    sect = lax.axis_index("sect")
    slab = lax.axis_index("slab")
    column = sect * slabs + slab
    columns = sects * slabs
    me = brick * sects + sect
    linear = me * slabs + slab
    everyone = peers * slabs

    row_order = (0, span_x - 1) + tuple(range(1, span_x - 1))
    row_loads = {
        x: pltpu.make_async_copy(
            geometry.at[:, pl.ds(x, 1)], geo.at[:, pl.ds(x, 1)], local_sem.at[8 + x]
        )
        for x in row_order
    }
    loads = [
        pltpu.make_async_copy(source, landing, local_sem.at[i])
        for i, (source, landing) in enumerate(
            (
                (place_in, place),
                (target_in, target),
                (kernels, taps),
                (attr_in, attr),
                (first, first_v),
                (middle, middle_v),
                (last_in, last),
            )
        )
    ]

    def inside(dx, dy):
        b, c = brick + dx, column + dy
        return (b >= 0) & (b < bricks) & (c >= 0) & (c < columns)

    near_only = bricks <= 4 and columns <= 4
    barrier = pltpu.get_barrier_semaphore()
    if near_only:
        for dx, dy in DIRECTIONS:
            @pl.when(inside(dx, dy))
            def _():
                pl.semaphore_signal(
                    barrier,
                    inc=1,
                    device_id={
                        "brick": brick + dx,
                        "sect": lax.div(column + dy, slabs),
                        "slab": lax.rem(column + dy, slabs),
                    },
                    device_id_type=MESH,
                )
        spread_x = 1 + (brick > 0).astype(jnp.int32) + (brick < bricks - 1).astype(jnp.int32)
        spread_y = 1 + (column > 0).astype(jnp.int32) + (column < columns - 1).astype(jnp.int32)
        expected = spread_x * spread_y - 1
    else:
        expected = everyone - 1
        for j in range(1, everyone):
            other = lax.rem(linear + j, everyone)
            pl.semaphore_signal(
                barrier,
                inc=1,
                device_id={
                    "brick": lax.div(other, columns),
                    "sect": lax.div(lax.rem(other, columns), slabs),
                    "slab": lax.rem(other, slabs),
                },
                device_id_type=MESH,
            )

    for x in row_order:
        row_loads[x].start()
    for load in loads:
        load.start()

    def remote(source, landing, phase, k):
        dx, dy = DIRECTIONS[k]
        c = column + dy
        return pltpu.make_async_remote_copy(
            src_ref=source,
            dst_ref=landing,
            send_sem=send_sem.at[phase, k],
            recv_sem=recv_sem.at[phase, k],
            device_id={"brick": brick + dx, "sect": lax.div(c, slabs), "slab": lax.rem(c, slabs)},
            device_id_type=MESH,
        )

    def halo_copy(phase, k):
        dx, dy = DIRECTIONS[k]
        if phase == 1 and dy == 0:
            return remote(partial.at[k], incoming.at[k], phase, k)
        if phase == 0 and dy == 0:
            row = pl.ds(span_x - 1 if dx == 1 else 0, 1)
            return remote(geometry.at[:, row], edge.at[k], phase, k)
        if phase == 2:
            return remote(place, near_place.at[k], phase, k)
        buffer = (pad, lat)[phase]
        return remote(
            buffer.at[send_range(dx, span_x), send_range(dy, span_y)],
            buffer.at[land_range(dx, span_x), land_range(dy, span_y)],
            phase,
            k,
        )

    def start(phase, which):
        for k in which:
            @pl.when(inside(*DIRECTIONS[k]))
            def _():
                halo_copy(phase, k).start()

    def land(phase, which):
        for k in which:
            dx, dy = DIRECTIONS[k]

            @pl.when(inside(-dx, -dy))
            def _():
                halo_copy(phase, k).wait_recv()

    def drain(phase, which):
        for k in which:
            @pl.when(inside(*DIRECTIONS[k]))
            def _():
                halo_copy(phase, k).wait_send()

    def turn(x, source):
        base = x * channels * span_y
        wide[base:base + channels * span_y] = source.astype(jnp.float32).reshape(
            channels * span_y, span_z
        )
        for y in range(span_y):
            pad[x, y + 1] = wide[pl.ds(base + y, channels, stride=span_y), :].astype(jnp.bfloat16)

    cells = lax.broadcasted_iota(jnp.int32, (span_z, count), 0).astype(jnp.float32) + 0.5

    def weights(points):
        local_x = points[0:1, :] * span_x
        local_y = points[1:2, :] * span_y
        local_z = points[2:3, :] * span_z
        return (
            [hat(local_x - (x - 0.5)) for x in range(span_x + 2)],
            [hat(local_y - (y - 0.5)) for y in range(span_y + 2)],
            hat(local_z - cells).astype(jnp.bfloat16),
        )

    pl.semaphore_wait(barrier, expected)
    start(0, (0, 1))
    loads[0].wait()
    start(2, (0, 1))
    for x in row_order[:2]:
        row_loads[x].wait()
        turn(x + 1, geo[:, x])
    start(0, range(2, 6))
    for x in row_order[2:]:
        row_loads[x].wait()
        turn(x + 1, geo[:, x])
    start(0, (6, 7))

    for k, (dx, dy) in enumerate(DIRECTIONS):
        @pl.when(jnp.logical_not(inside(-dx, -dy)))
        def _():
            if dy != 0:
                for buffer in (pad, lat):
                    region = buffer.at[land_range(dx, span_x), land_range(dy, span_y)]
                    region[...] = jnp.zeros(region.shape, jnp.bfloat16)
            else:
                edge[k] = jnp.zeros(edge.shape[1:], jnp.bfloat16)
                near_place[k] = jnp.zeros(near_place.shape[1:], jnp.float32)
                incoming[k] = jnp.zeros(incoming.shape[1:], jnp.bfloat16)

    loads[2].wait()
    for a in range(3):
        for b in range(3):
            for e in range(3):
                tap = taps[0, a, b, e].astype(jnp.float32).T.astype(jnp.bfloat16)
                low = (a * 3 + b) * channels
                taps_t[e * channels:(e + 1) * channels, low:low + channels] = tap

    lane = lax.broadcasted_iota(jnp.int32, (channels, span_z), 1)

    def product(x, y, low, high):
        near = jnp.concatenate(
            [
                jnp.concatenate(
                    [pad[x + a, y + i:y + i + 3].reshape(3 * channels, span_z) for i in (0, 1)],
                    axis=1,
                )
                for a in range(low, high)
            ],
            axis=0,
        )
        return dot(taps_t[:, low * 3 * channels:high * 3 * channels], near)

    def finish(x, y, pair):
        for i in (0, 1):
            part = pair[:, i * span_z:(i + 1) * span_z]
            left = pltpu.roll(part[:channels], 1, 1)
            right = pltpu.roll(part[2 * channels:], span_z - 1, 1)
            response = (
                part[channels:2 * channels]
                + jnp.where(lane == 0, 0.0, left)
                + jnp.where(lane == span_z - 1, 0.0, right)
            )
            old = pad[x + 1, y + i + 1].astype(jnp.float32)
            lat[x + 1, y + i + 1] = (old + gelu(response)).astype(jnp.bfloat16)

    early = {}

    def inner_rows(some):
        for x in range(1, span_x - 1):
            for y in some:
                finish(x, y, product(x, y, 0, 3))
        for x, low, high in ((0, 1, 3), (span_x - 1, 0, 2)):
            for y in some:
                early[x, y] = product(x, y, low, high)

    inner_rows(range(2, span_y - 2, 2))
    land(0, (6, 7))
    inner_rows((0, span_y - 2))
    land(2, (0, 1))
    theirs = [weights(near_place.at[1 - k]) for k in (0, 1)]
    land(0, (0, 1))
    turn(0, edge[0, :, 0])
    turn(span_x + 1, edge[1, :, 0])

    def outer_rows(some):
        for y in some:
            for x, a in ((0, 0), (span_x - 1, 2)):
                finish(x, y, early[x, y] + product(x, y, a, a + 1))

    outer_rows(range(2, span_y - 2, 2))
    land(0, range(2, 6))
    outer_rows((0, span_y - 2))
    start(1, range(2, 8))

    def sample(of_weights, x, weight, low, high):
        weight_y, weight_z = of_weights[1:]
        part = dot(lat[x, low:high].reshape((high - low) * channels, span_z), weight_z)
        inner = None
        for y in range(low, high):
            term = part[(y - low) * channels:(y - low + 1) * channels] * weight_y[y]
            inner = term if inner is None else inner + term
        return inner * weight

    for k, x, weight in ((0, span_x, 0), (1, 1, span_x + 1)):
        weight_x = theirs[k][0][weight]
        partial[k] = sample(theirs[k], x, weight_x, 1, span_y + 1).astype(jnp.bfloat16)
        start(1, (k,))

    own_weights = weights(place)

    loads[1].wait()
    named = lax.broadcasted_iota(jnp.int32, (peers, count), 0)
    onehot = named == target[...]
    earlier = lax.broadcasted_iota(jnp.int32, (count, count), 0) < lax.broadcasted_iota(
        jnp.int32, (count, count), 1
    )
    before = dot(onehot.astype(jnp.bfloat16), earlier.astype(jnp.bfloat16))
    named_brick = lax.div(named, jnp.int32(sects))
    named_sect = named - named_brick * sects
    upper = (named_sect >= sects // 2).astype(jnp.int32)
    block = upper * (peers // 2) + named_brick * (sects // 2) + named_sect - upper * (sects // 2)
    position = jnp.sum(
        jnp.where(onehot, before + (block * cap).astype(jnp.float32), 0.0), axis=0, keepdims=True
    )
    slots = lax.broadcasted_iota(jnp.int32, (2 * half, count), 0)
    gather = (slots == position.astype(jnp.int32)).astype(jnp.bfloat16)


    outbox[...] = jnp.zeros(outbox.shape, jnp.float32)
    weight_x, weight_y, weight_z = own_weights
    total = None
    for x in range(1, span_x + 1):
        term = sample(own_weights, x, weight_x[x], 1, span_y + 1)
        total = term if total is None else total + term
    land(1, range(2, 8))
    for y in (0, span_y + 1):
        part = dot(lat[:, y].reshape((span_x + 2) * channels, span_z), weight_z)
        inner = part[:channels] * weight_x[0]
        for x in range(1, span_x + 2):
            inner = inner + part[x * channels:(x + 1) * channels] * weight_x[x]
        total = total + inner * weight_y[y]
    for load in loads[3:]:
        load.wait()
    land(1, (0, 1))
    total = total + incoming[0].astype(jnp.float32) + incoming[1].astype(jnp.float32)
    row = jnp.concatenate([total.astype(jnp.bfloat16), attr[...]], axis=0)
    table = lax.dot_general(gather, row, NT, preferred_element_type=jnp.float32)
    table = table.astype(jnp.bfloat16)

    acts = [
        gelu(dot(table[s * half:(s + 1) * half], first_v[s])).astype(jnp.bfloat16) for s in range(2)
    ]
    for layer in range(middle_v.shape[1]):
        acts = [gelu(dot(acts[s], middle_v[s, layer])).astype(jnp.bfloat16) for s in range(2)]
    for s in range(2):
        value = lax.dot_general(last[s], acts[s], NT, preferred_element_type=jnp.float32)
        outbox[s, 0:value.shape[0], 0:half] = value

    def value_copy(j):
        other = lax.rem(me + j, peers)
        there = lax.rem(other, sects)
        return pltpu.make_async_remote_copy(
            src_ref=outbox.at[lax.div(there, sects // 2)],
            dst_ref=inbox.at[me],
            send_sem=value_send.at[j],
            recv_sem=value_recv.at[j],
            device_id={"brick": lax.div(other, sects), "sect": there},
            device_id_type=MESH,
        )

    for j in range(1, peers):
        value_copy(j).start()
    inbox[me] = outbox[lax.div(sect, sects // 2)]
    drain(0, range(8))
    drain(1, range(8))
    drain(2, (0, 1))
    for j in range(1, peers):
        value_copy(j).wait()

    width = inbox.shape[2]
    own = (brick * (sects // 2) + sect % (sects // 2)) * cap
    rolled = pltpu.roll(inbox[...].reshape(peers * 8, width), lax.rem(width - own, width), 1)
    for i in range(peers):
        out[:, i * cap:(i + 1) * cap] = rolled[i * 8:i * 8 + out.shape[0], 0:cap]


def on_device(
    sizes,
    geometry,
    conv_kernels,
    point_place,
    point_attr,
    destination,
    dense_first,
    dense_middle,
    dense_last,
):
    bricks, sects, slabs = sizes
    channels, span_x, span_y, span_z = geometry.shape
    count = point_place.shape[1]
    peers = bricks * sects
    cap = 5 * count // (4 * peers)
    width = -(-(peers // 2 * cap) // 128) * 128
    padded = (span_x + 2, span_y + 2, channels, span_z)
    attr = point_attr.T
    target = destination.reshape(1, count)
    return pl.pallas_call(
        functools.partial(kernel, bricks, sects, slabs),
        out_shape=pltpu.VMEM((dense_last.shape[1], peers * cap), jnp.float32),
        in_specs=[pl.BlockSpec(memory_space=pl.ANY)] * 8,
        out_specs=pl.BlockSpec(memory_space=pltpu.VMEM),
        scratch_shapes=[
            pltpu.VMEM(geometry.shape, jnp.bfloat16),
            pltpu.VMEM(((span_x + 2) * channels * span_y, span_z), jnp.float32),
            pltpu.VMEM(padded, jnp.bfloat16),
            pltpu.VMEM(padded, jnp.bfloat16),
            pltpu.VMEM(conv_kernels.shape, jnp.bfloat16),
            pltpu.VMEM((3 * channels, 9 * channels), jnp.bfloat16),
            pltpu.VMEM(point_place.shape, jnp.float32),
            pltpu.VMEM(attr.shape, jnp.bfloat16),
            pltpu.VMEM(target.shape, jnp.int32),
            pltpu.VMEM(dense_first.shape, jnp.bfloat16),
            pltpu.VMEM(dense_middle.shape, jnp.bfloat16),
            pltpu.VMEM(dense_last.shape, jnp.bfloat16),
            pltpu.VMEM((2,) + point_place.shape, jnp.float32),
            pltpu.VMEM((2, channels, count), jnp.bfloat16),
            pltpu.VMEM((2, channels, count), jnp.bfloat16),
            pltpu.VMEM((2, channels, 1, span_y, span_z), jnp.bfloat16),
            pltpu.VMEM((2, 8, width), jnp.float32),
            pltpu.VMEM((peers, 8, width), jnp.float32),
            pltpu.SemaphoreType.DMA((8 + span_x,)),
            pltpu.SemaphoreType.DMA((3, 8)),
            pltpu.SemaphoreType.DMA((3, 8)),
            pltpu.SemaphoreType.DMA((peers,)),
            pltpu.SemaphoreType.DMA((peers,)),
        ],
        compiler_params=pltpu.CompilerParams(
            collective_id=0, has_side_effects=True, vmem_limit_bytes=60 * 2**20
        ),
    )(
        geometry,
        conv_kernels,
        point_place,
        attr,
        target,
        dense_first,
        dense_middle,
        dense_last,
    )


def solution(mesh):
    sizes = tuple(mesh.shape[axis] for axis in ("brick", "sect", "slab"))
    in_specs = (
        P(None, ("case", "brick"), ("sect", "slab"), None),
        P(),
        P(None, ("case", "brick", "sect", "slab")),
        P(("case", "brick", "sect", "slab"), None),
        P(("case", "brick", "sect", "slab"), None),
        P(),
        P(),
        P(),
    )
    out_specs = P(None, ("case", "brick", "sect", "slab"))
    return jax.shard_map(
        functools.partial(on_device, sizes),
        mesh=mesh,
        in_specs=in_specs,
        out_specs=out_specs,
        check_vma=False,
    )
```

```python
import functools
import math

import jax
import jax.numpy as jnp
from jax import lax
from jax.experimental import pallas as pl
from jax.experimental.pallas import tpu as pltpu
from jax.sharding import PartitionSpec as P

MESH = pl.DeviceIdType.MESH
DIRECTIONS = ((1, 0), (-1, 0), (1, 1), (1, -1), (-1, 1), (-1, -1), (0, 1), (0, -1))
NT = (((1,), (1,)), ((), ()))


def hat(offset):
    return jnp.maximum(0.0, 1.0 - jnp.abs(offset))


def gelu(value):
    scale = (2.0 / math.pi) ** 0.5
    middle = 0.5 * value
    return middle + middle * jnp.tanh(value * (scale + (scale * 0.044715) * (value * value)))


def dot(a, b):
    return jnp.dot(a, b, preferred_element_type=jnp.float32)


def send_range(step, size):
    return {1: pl.ds(size, 1), -1: pl.ds(1, 1), 0: pl.ds(1, size)}[step]


def land_range(step, size):
    return {1: pl.ds(0, 1), -1: pl.ds(size + 1, 1), 0: pl.ds(1, size)}[step]


def kernel(
    bricks,
    sects,
    slabs,
    geometry,
    kernels,
    place_in,
    attr_in,
    target_in,
    first,
    middle,
    last_in,
    out,
    geo,
    wide,
    pad,
    lat,
    taps,
    taps_t,
    place,
    attr,
    target,
    first_v,
    middle_v,
    last,
    near_place,
    partial,
    incoming,
    edge,
    outbox,
    inbox,
    local_sem,
    send_sem,
    recv_sem,
    value_send,
    value_recv,
):
    channels, span_x, span_y, span_z = geo.shape
    count = place.shape[1]
    peers = bricks * sects
    cap = 5 * count // (4 * peers)
    half = peers // 2 * cap
    brick = lax.axis_index("brick")
    sect = lax.axis_index("sect")
    slab = lax.axis_index("slab")
    column = sect * slabs + slab
    columns = sects * slabs
    me = brick * sects + sect
    linear = me * slabs + slab
    everyone = peers * slabs

    row_order = (0, span_x - 1) + tuple(range(1, span_x - 1))
    row_loads = {
        x: pltpu.make_async_copy(
            geometry.at[:, pl.ds(x, 1)], geo.at[:, pl.ds(x, 1)], local_sem.at[8 + x]
        )
        for x in row_order
    }
    loads = [
        pltpu.make_async_copy(source, landing, local_sem.at[i])
        for i, (source, landing) in enumerate(
            (
                (place_in, place),
                (target_in, target),
                (kernels, taps),
                (attr_in, attr),
                (first, first_v),
                (middle, middle_v),
                (last_in, last),
            )
        )
    ]

    def inside(dx, dy):
        b, c = brick + dx, column + dy
        return (b >= 0) & (b < bricks) & (c >= 0) & (c < columns)

    near_only = bricks <= 4 and columns <= 4
    barrier = pltpu.get_barrier_semaphore()
    if near_only:
        for dx, dy in DIRECTIONS:
            @pl.when(inside(dx, dy))
            def _():
                pl.semaphore_signal(
                    barrier,
                    inc=1,
                    device_id={
                        "brick": brick + dx,
                        "sect": lax.div(column + dy, slabs),
                        "slab": lax.rem(column + dy, slabs),
                    },
                    device_id_type=MESH,
                )
        spread_x = 1 + (brick > 0).astype(jnp.int32) + (brick < bricks - 1).astype(jnp.int32)
        spread_y = 1 + (column > 0).astype(jnp.int32) + (column < columns - 1).astype(jnp.int32)
        expected = spread_x * spread_y - 1
    else:
        expected = everyone - 1
        for j in range(1, everyone):
            other = lax.rem(linear + j, everyone)
            pl.semaphore_signal(
                barrier,
                inc=1,
                device_id={
                    "brick": lax.div(other, columns),
                    "sect": lax.div(lax.rem(other, columns), slabs),
                    "slab": lax.rem(other, slabs),
                },
                device_id_type=MESH,
            )

    for x in row_order:
        row_loads[x].start()
    for load in loads:
        load.start()

    def remote(source, landing, phase, k):
        dx, dy = DIRECTIONS[k]
        c = column + dy
        return pltpu.make_async_remote_copy(
            src_ref=source,
            dst_ref=landing,
            send_sem=send_sem.at[phase, k],
            recv_sem=recv_sem.at[phase, k],
            device_id={"brick": brick + dx, "sect": lax.div(c, slabs), "slab": lax.rem(c, slabs)},
            device_id_type=MESH,
        )

    middle_c = channels // 2

    def halo_copy(phase, k):
        dx, dy = DIRECTIONS[k]
        if phase == 1 and dy == 0:
            return remote(partial.at[k], incoming.at[k], phase, k)
        if phase == 0 and dy == 0:
            row = pl.ds(span_x - 1 if dx == 1 else 0, 1)
            return remote(geometry.at[:middle_c, row], edge.at[k, :middle_c], phase, k)
        if phase == 3:
            row = pl.ds(span_x - 1 if dx == 1 else 0, 1)
            return remote(geometry.at[middle_c:, row], edge.at[k, middle_c:], phase, k)
        if phase == 2:
            return remote(place, near_place.at[k], phase, k)
        buffer = (pad, lat)[phase]
        return remote(
            buffer.at[send_range(dx, span_x), send_range(dy, span_y)],
            buffer.at[land_range(dx, span_x), land_range(dy, span_y)],
            phase,
            k,
        )

    def start(phase, which):
        for k in which:
            @pl.when(inside(*DIRECTIONS[k]))
            def _():
                halo_copy(phase, k).start()

    def land(phase, which):
        for k in which:
            dx, dy = DIRECTIONS[k]

            @pl.when(inside(-dx, -dy))
            def _():
                halo_copy(phase, k).wait_recv()

    def drain(phase, which):
        for k in which:
            @pl.when(inside(*DIRECTIONS[k]))
            def _():
                halo_copy(phase, k).wait_send()

    def turn(x, source, first_c=0):
        size = source.shape[0]
        base = (x * channels + first_c) * span_y
        wide[base:base + size * span_y] = source.astype(jnp.float32).reshape(size * span_y, span_z)
        for y in range(span_y):
            turned = wide[pl.ds(base + y, size, stride=span_y), :].astype(jnp.bfloat16)
            pad[x, y + 1, first_c:first_c + size] = turned

    cells = lax.broadcasted_iota(jnp.int32, (span_z, count), 0).astype(jnp.float32) + 0.5

    def weights(points):
        local_x = points[0:1, :] * span_x
        local_y = points[1:2, :] * span_y
        local_z = points[2:3, :] * span_z
        return (
            [hat(local_x - (x - 0.5)) for x in range(span_x + 2)],
            [hat(local_y - (y - 0.5)) for y in range(span_y + 2)],
            hat(local_z - cells).astype(jnp.bfloat16),
        )

    pl.semaphore_wait(barrier, expected)
    start(0, (0, 1))
    start(3, (0, 1))
    loads[0].wait()
    start(2, (0, 1))
    for x in row_order[:2]:
        row_loads[x].wait()
        turn(x + 1, geo[:, x])
    start(0, range(2, 6))
    for x in row_order[2:]:
        row_loads[x].wait()
        turn(x + 1, geo[:, x])
    start(0, (6, 7))

    for k, (dx, dy) in enumerate(DIRECTIONS):
        @pl.when(jnp.logical_not(inside(-dx, -dy)))
        def _():
            if dy != 0:
                for buffer in (pad, lat):
                    region = buffer.at[land_range(dx, span_x), land_range(dy, span_y)]
                    region[...] = jnp.zeros(region.shape, jnp.bfloat16)
            else:
                edge[k] = jnp.zeros(edge.shape[1:], jnp.bfloat16)
                near_place[k] = jnp.zeros(near_place.shape[1:], jnp.float32)
                incoming[k] = jnp.zeros(incoming.shape[1:], jnp.bfloat16)

    loads[2].wait()
    for a in range(3):
        for b in range(3):
            for e in range(3):
                tap = taps[0, a, b, e].astype(jnp.float32).T.astype(jnp.bfloat16)
                low = (a * 3 + b) * channels
                taps_t[e * channels:(e + 1) * channels, low:low + channels] = tap

    lane = lax.broadcasted_iota(jnp.int32, (channels, span_z), 1)

    def product(x, y, low, high):
        near = jnp.concatenate(
            [
                jnp.concatenate(
                    [pad[x + a, y + i:y + i + 3].reshape(3 * channels, span_z) for i in (0, 1)],
                    axis=1,
                )
                for a in range(low, high)
            ],
            axis=0,
        )
        return dot(taps_t[:, low * 3 * channels:high * 3 * channels], near)

    def finish(x, y, pair):
        for i in (0, 1):
            part = pair[:, i * span_z:(i + 1) * span_z]
            left = pltpu.roll(part[:channels], 1, 1)
            right = pltpu.roll(part[2 * channels:], span_z - 1, 1)
            response = (
                part[channels:2 * channels]
                + jnp.where(lane == 0, 0.0, left)
                + jnp.where(lane == span_z - 1, 0.0, right)
            )
            old = pad[x + 1, y + i + 1].astype(jnp.float32)
            lat[x + 1, y + i + 1] = (old + gelu(response)).astype(jnp.bfloat16)

    early = {}

    def inner_rows(some):
        for x in range(1, span_x - 1):
            for y in some:
                finish(x, y, product(x, y, 0, 3))
        for x, low, high in ((0, 1, 3), (span_x - 1, 0, 2)):
            for y in some:
                early[x, y] = product(x, y, low, high)

    inner_rows(range(2, span_y - 2, 2))
    land(0, (6, 7))
    inner_rows((0, span_y - 2))
    land(2, (0, 1))
    theirs = [weights(near_place.at[1 - k]) for k in (0, 1)]
    for phase, first_c in ((0, 0), (3, middle_c)):
        land(phase, (0, 1))
        turn(0, edge[0, first_c:first_c + middle_c, 0], first_c)
        turn(span_x + 1, edge[1, first_c:first_c + middle_c, 0], first_c)

    def outer_rows(some):
        for y in some:
            for x, a in ((0, 0), (span_x - 1, 2)):
                finish(x, y, early[x, y] + product(x, y, a, a + 1))

    outer_rows(range(2, span_y - 2, 2))
    land(0, range(2, 6))
    outer_rows((0, span_y - 2))
    start(1, range(2, 8))

    def sample(of_weights, x, weight, low, high):
        weight_y, weight_z = of_weights[1:]
        part = dot(lat[x, low:high].reshape((high - low) * channels, span_z), weight_z)
        inner = None
        for y in range(low, high):
            term = part[(y - low) * channels:(y - low + 1) * channels] * weight_y[y]
            inner = term if inner is None else inner + term
        return inner * weight

    for k, x, weight in ((0, span_x, 0), (1, 1, span_x + 1)):
        weight_x = theirs[k][0][weight]
        partial[k] = sample(theirs[k], x, weight_x, 1, span_y + 1).astype(jnp.bfloat16)
        start(1, (k,))

    own_weights = weights(place)

    loads[1].wait()
    named = lax.broadcasted_iota(jnp.int32, (peers, count), 0)
    onehot = named == target[...]
    earlier = lax.broadcasted_iota(jnp.int32, (count, count), 0) < lax.broadcasted_iota(
        jnp.int32, (count, count), 1
    )
    before = dot(onehot.astype(jnp.bfloat16), earlier.astype(jnp.bfloat16))
    named_brick = lax.div(named, jnp.int32(sects))
    named_sect = named - named_brick * sects
    upper = (named_sect >= sects // 2).astype(jnp.int32)
    block = upper * (peers // 2) + named_brick * (sects // 2) + named_sect - upper * (sects // 2)
    position = jnp.sum(
        jnp.where(onehot, before + (block * cap).astype(jnp.float32), 0.0), axis=0, keepdims=True
    )
    slots = lax.broadcasted_iota(jnp.int32, (2 * half, count), 0)
    gather = (slots == position.astype(jnp.int32)).astype(jnp.bfloat16)


    outbox[...] = jnp.zeros(outbox.shape, jnp.float32)
    weight_x, weight_y, weight_z = own_weights
    total = None
    for x in range(1, span_x + 1):
        term = sample(own_weights, x, weight_x[x], 1, span_y + 1)
        total = term if total is None else total + term
    land(1, range(2, 8))
    for y in (0, span_y + 1):
        part = dot(lat[:, y].reshape((span_x + 2) * channels, span_z), weight_z)
        inner = part[:channels] * weight_x[0]
        for x in range(1, span_x + 2):
            inner = inner + part[x * channels:(x + 1) * channels] * weight_x[x]
        total = total + inner * weight_y[y]
    for load in loads[3:]:
        load.wait()
    land(1, (0, 1))
    total = total + incoming[0].astype(jnp.float32) + incoming[1].astype(jnp.float32)
    row = jnp.concatenate([total.astype(jnp.bfloat16), attr[...]], axis=0)
    table = lax.dot_general(gather, row, NT, preferred_element_type=jnp.float32)
    table = table.astype(jnp.bfloat16)

    acts = [
        gelu(dot(table[s * half:(s + 1) * half], first_v[s])).astype(jnp.bfloat16) for s in range(2)
    ]
    for layer in range(middle_v.shape[1]):
        acts = [gelu(dot(acts[s], middle_v[s, layer])).astype(jnp.bfloat16) for s in range(2)]
    for s in range(2):
        value = lax.dot_general(last[s], acts[s], NT, preferred_element_type=jnp.float32)
        outbox[s, 0:value.shape[0], 0:half] = value

    def value_copy(j):
        other = lax.rem(me + j, peers)
        there = lax.rem(other, sects)
        return pltpu.make_async_remote_copy(
            src_ref=outbox.at[lax.div(there, sects // 2)],
            dst_ref=inbox.at[me],
            send_sem=value_send.at[j],
            recv_sem=value_recv.at[j],
            device_id={"brick": lax.div(other, sects), "sect": there},
            device_id_type=MESH,
        )

    for j in range(1, peers):
        value_copy(j).start()
    inbox[me] = outbox[lax.div(sect, sects // 2)]
    drain(0, range(8))
    drain(1, range(8))
    drain(2, (0, 1))
    drain(3, (0, 1))
    for j in range(1, peers):
        value_copy(j).wait()

    width = inbox.shape[2]
    own = (brick * (sects // 2) + sect % (sects // 2)) * cap
    rolled = pltpu.roll(inbox[...].reshape(peers * 8, width), lax.rem(width - own, width), 1)
    for i in range(peers):
        out[:, i * cap:(i + 1) * cap] = rolled[i * 8:i * 8 + out.shape[0], 0:cap]


def on_device(
    sizes,
    geometry,
    conv_kernels,
    point_place,
    point_attr,
    destination,
    dense_first,
    dense_middle,
    dense_last,
):
    bricks, sects, slabs = sizes
    channels, span_x, span_y, span_z = geometry.shape
    count = point_place.shape[1]
    peers = bricks * sects
    cap = 5 * count // (4 * peers)
    width = -(-(peers // 2 * cap) // 128) * 128
    padded = (span_x + 2, span_y + 2, channels, span_z)
    attr = point_attr.T
    target = destination.reshape(1, count)
    return pl.pallas_call(
        functools.partial(kernel, bricks, sects, slabs),
        out_shape=pltpu.VMEM((dense_last.shape[1], peers * cap), jnp.float32),
        in_specs=[pl.BlockSpec(memory_space=pl.ANY)] * 8,
        out_specs=pl.BlockSpec(memory_space=pltpu.VMEM),
        scratch_shapes=[
            pltpu.VMEM(geometry.shape, jnp.bfloat16),
            pltpu.VMEM(((span_x + 2) * channels * span_y, span_z), jnp.float32),
            pltpu.VMEM(padded, jnp.bfloat16),
            pltpu.VMEM(padded, jnp.bfloat16),
            pltpu.VMEM(conv_kernels.shape, jnp.bfloat16),
            pltpu.VMEM((3 * channels, 9 * channels), jnp.bfloat16),
            pltpu.VMEM(point_place.shape, jnp.float32),
            pltpu.VMEM(attr.shape, jnp.bfloat16),
            pltpu.VMEM(target.shape, jnp.int32),
            pltpu.VMEM(dense_first.shape, jnp.bfloat16),
            pltpu.VMEM(dense_middle.shape, jnp.bfloat16),
            pltpu.VMEM(dense_last.shape, jnp.bfloat16),
            pltpu.VMEM((2,) + point_place.shape, jnp.float32),
            pltpu.VMEM((2, channels, count), jnp.bfloat16),
            pltpu.VMEM((2, channels, count), jnp.bfloat16),
            pltpu.VMEM((2, channels, 1, span_y, span_z), jnp.bfloat16),
            pltpu.VMEM((2, 8, width), jnp.float32),
            pltpu.VMEM((peers, 8, width), jnp.float32),
            pltpu.SemaphoreType.DMA((8 + span_x,)),
            pltpu.SemaphoreType.DMA((4, 8)),
            pltpu.SemaphoreType.DMA((4, 8)),
            pltpu.SemaphoreType.DMA((peers,)),
            pltpu.SemaphoreType.DMA((peers,)),
        ],
        compiler_params=pltpu.CompilerParams(
            collective_id=0, has_side_effects=True, vmem_limit_bytes=60 * 2**20
        ),
    )(
        geometry,
        conv_kernels,
        point_place,
        attr,
        target,
        dense_first,
        dense_middle,
        dense_last,
    )


def solution(mesh):
    sizes = tuple(mesh.shape[axis] for axis in ("brick", "sect", "slab"))
    in_specs = (
        P(None, ("case", "brick"), ("sect", "slab"), None),
        P(),
        P(None, ("case", "brick", "sect", "slab")),
        P(("case", "brick", "sect", "slab"), None),
        P(("case", "brick", "sect", "slab"), None),
        P(),
        P(),
        P(),
    )
    out_specs = P(None, ("case", "brick", "sect", "slab"))
    return jax.shard_map(
        functools.partial(on_device, sizes),
        mesh=mesh,
        in_specs=in_specs,
        out_specs=out_specs,
        check_vma=False,
    )
```

```python
import functools
import math

import jax
import jax.numpy as jnp
from jax import lax
from jax.experimental import pallas as pl
from jax.experimental.pallas import tpu as pltpu
from jax.sharding import PartitionSpec as P

MESH = pl.DeviceIdType.MESH
DIRECTIONS = ((1, 0), (-1, 0), (1, 1), (1, -1), (-1, 1), (-1, -1), (0, 1), (0, -1))
NT = (((1,), (1,)), ((), ()))


def hat(offset):
    return jnp.maximum(0.0, 1.0 - jnp.abs(offset))


def gelu(value):
    scale = (2.0 / math.pi) ** 0.5
    middle = 0.5 * value
    return middle + middle * jnp.tanh(value * (scale + (scale * 0.044715) * (value * value)))


def dot(a, b):
    return jnp.dot(a, b, preferred_element_type=jnp.float32)


def send_range(step, size):
    return {1: pl.ds(size, 1), -1: pl.ds(1, 1), 0: pl.ds(1, size)}[step]


def land_range(step, size):
    return {1: pl.ds(0, 1), -1: pl.ds(size + 1, 1), 0: pl.ds(1, size)}[step]


def kernel(
    bricks,
    sects,
    slabs,
    geometry,
    kernels,
    place_in,
    attr_in,
    target_in,
    first,
    middle,
    last_in,
    out,
    geo,
    wide,
    pad,
    lat,
    taps,
    taps_t,
    place,
    attr,
    target,
    first_v,
    middle_v,
    last,
    near_place,
    partial,
    incoming,
    edge,
    outbox,
    inbox,
    local_sem,
    send_sem,
    recv_sem,
    value_send,
    value_recv,
):
    channels, span_x, span_y, span_z = geo.shape
    count = place.shape[1]
    peers = bricks * sects
    cap = 5 * count // (4 * peers)
    half = peers // 2 * cap
    brick = lax.axis_index("brick")
    sect = lax.axis_index("sect")
    slab = lax.axis_index("slab")
    column = sect * slabs + slab
    columns = sects * slabs
    me = brick * sects + sect
    linear = me * slabs + slab
    everyone = peers * slabs

    row_order = (0, span_x - 1) + tuple(range(1, span_x - 1))
    row_loads = {
        x: pltpu.make_async_copy(
            geometry.at[:, pl.ds(x, 1)], geo.at[:, pl.ds(x, 1)], local_sem.at[8 + x]
        )
        for x in row_order
    }
    loads = [
        pltpu.make_async_copy(source, landing, local_sem.at[i])
        for i, (source, landing) in enumerate(
            (
                (place_in, place),
                (target_in, target),
                (kernels, taps),
                (attr_in, attr),
                (first, first_v),
                (middle, middle_v),
                (last_in, last),
            )
        )
    ]

    def inside(dx, dy):
        b, c = brick + dx, column + dy
        return (b >= 0) & (b < bricks) & (c >= 0) & (c < columns)

    near_only = bricks <= 4 and columns <= 4
    barrier = pltpu.get_barrier_semaphore()
    if near_only:
        for dx, dy in DIRECTIONS:
            @pl.when(inside(dx, dy))
            def _():
                pl.semaphore_signal(
                    barrier,
                    inc=1,
                    device_id={
                        "brick": brick + dx,
                        "sect": lax.div(column + dy, slabs),
                        "slab": lax.rem(column + dy, slabs),
                    },
                    device_id_type=MESH,
                )
        spread_x = 1 + (brick > 0).astype(jnp.int32) + (brick < bricks - 1).astype(jnp.int32)
        spread_y = 1 + (column > 0).astype(jnp.int32) + (column < columns - 1).astype(jnp.int32)
        expected = spread_x * spread_y - 1
    else:
        expected = everyone - 1
        for j in range(1, everyone):
            other = lax.rem(linear + j, everyone)
            pl.semaphore_signal(
                barrier,
                inc=1,
                device_id={
                    "brick": lax.div(other, columns),
                    "sect": lax.div(lax.rem(other, columns), slabs),
                    "slab": lax.rem(other, slabs),
                },
                device_id_type=MESH,
            )

    for x in row_order:
        row_loads[x].start()
    for load in loads:
        load.start()

    def remote(source, landing, phase, k):
        dx, dy = DIRECTIONS[k]
        c = column + dy
        return pltpu.make_async_remote_copy(
            src_ref=source,
            dst_ref=landing,
            send_sem=send_sem.at[phase, k],
            recv_sem=recv_sem.at[phase, k],
            device_id={"brick": brick + dx, "sect": lax.div(c, slabs), "slab": lax.rem(c, slabs)},
            device_id_type=MESH,
        )

    def halo_copy(phase, k):
        dx, dy = DIRECTIONS[k]
        if phase == 1 and dy == 0:
            return remote(partial.at[k], incoming.at[k], phase, k)
        if phase == 0 and dy == 0:
            row = pl.ds(span_x - 1 if dx == 1 else 0, 1)
            return remote(geometry.at[:, row], edge.at[k], phase, k)
        if phase == 2:
            return remote(place, near_place.at[k], phase, k)
        buffer = (pad, lat)[phase]
        return remote(
            buffer.at[send_range(dx, span_x), send_range(dy, span_y)],
            buffer.at[land_range(dx, span_x), land_range(dy, span_y)],
            phase,
            k,
        )

    def start(phase, which):
        for k in which:
            @pl.when(inside(*DIRECTIONS[k]))
            def _():
                halo_copy(phase, k).start()

    def land(phase, which):
        for k in which:
            dx, dy = DIRECTIONS[k]

            @pl.when(inside(-dx, -dy))
            def _():
                halo_copy(phase, k).wait_recv()

    def drain(phase, which):
        for k in which:
            @pl.when(inside(*DIRECTIONS[k]))
            def _():
                halo_copy(phase, k).wait_send()

    def turn(x, source):
        base = x * channels * span_y
        wide[base:base + channels * span_y] = source.astype(jnp.float32).reshape(
            channels * span_y, span_z
        )
        for y in range(span_y):
            pad[x, y + 1] = wide[pl.ds(base + y, channels, stride=span_y), :].astype(jnp.bfloat16)

    cells = lax.broadcasted_iota(jnp.int32, (span_z, count), 0).astype(jnp.float32) + 0.5

    def weights(points):
        local_x = points[0:1, :] * span_x
        local_y = points[1:2, :] * span_y
        local_z = points[2:3, :] * span_z
        return (
            [hat(local_x - (x - 0.5)) for x in range(span_x + 2)],
            [hat(local_y - (y - 0.5)) for y in range(span_y + 2)],
            hat(local_z - cells).astype(jnp.bfloat16),
        )

    pl.semaphore_wait(barrier, expected)
    start(0, (0, 1))
    loads[0].wait()
    start(2, (0, 1))
    own_weights = weights(place)

    loads[1].wait()
    named = lax.broadcasted_iota(jnp.int32, (peers, count), 0)
    onehot = named == target[...]
    earlier = lax.broadcasted_iota(jnp.int32, (count, count), 0) < lax.broadcasted_iota(
        jnp.int32, (count, count), 1
    )
    before = dot(onehot.astype(jnp.bfloat16), earlier.astype(jnp.bfloat16))
    named_brick = lax.div(named, jnp.int32(sects))
    named_sect = named - named_brick * sects
    upper = (named_sect >= sects // 2).astype(jnp.int32)
    block = upper * (peers // 2) + named_brick * (sects // 2) + named_sect - upper * (sects // 2)
    position = jnp.sum(
        jnp.where(onehot, before + (block * cap).astype(jnp.float32), 0.0), axis=0, keepdims=True
    )
    slots = lax.broadcasted_iota(jnp.int32, (2 * half, count), 0)
    gather = (slots == position.astype(jnp.int32)).astype(jnp.bfloat16)

    for x in row_order[:2]:
        row_loads[x].wait()
        turn(x + 1, geo[:, x])
    start(0, range(2, 6))
    for x in row_order[2:]:
        row_loads[x].wait()
        turn(x + 1, geo[:, x])
    start(0, (6, 7))

    for k, (dx, dy) in enumerate(DIRECTIONS):
        @pl.when(jnp.logical_not(inside(-dx, -dy)))
        def _():
            if dy != 0:
                for buffer in (pad, lat):
                    region = buffer.at[land_range(dx, span_x), land_range(dy, span_y)]
                    region[...] = jnp.zeros(region.shape, jnp.bfloat16)
            else:
                edge[k] = jnp.zeros(edge.shape[1:], jnp.bfloat16)
                near_place[k] = jnp.zeros(near_place.shape[1:], jnp.float32)
                incoming[k] = jnp.zeros(incoming.shape[1:], jnp.bfloat16)

    loads[2].wait()
    for a in range(3):
        for b in range(3):
            for e in range(3):
                tap = taps[0, a, b, e].astype(jnp.float32).T.astype(jnp.bfloat16)
                low = (a * 3 + b) * channels
                taps_t[e * channels:(e + 1) * channels, low:low + channels] = tap

    lane = lax.broadcasted_iota(jnp.int32, (channels, span_z), 1)

    def product(x, y, low, high):
        near = jnp.concatenate(
            [
                jnp.concatenate(
                    [pad[x + a, y + i:y + i + 3].reshape(3 * channels, span_z) for i in (0, 1)],
                    axis=1,
                )
                for a in range(low, high)
            ],
            axis=0,
        )
        return dot(taps_t[:, low * 3 * channels:high * 3 * channels], near)

    def finish(x, y, pair):
        for i in (0, 1):
            part = pair[:, i * span_z:(i + 1) * span_z]
            left = pltpu.roll(part[:channels], 1, 1)
            right = pltpu.roll(part[2 * channels:], span_z - 1, 1)
            response = (
                part[channels:2 * channels]
                + jnp.where(lane == 0, 0.0, left)
                + jnp.where(lane == span_z - 1, 0.0, right)
            )
            old = pad[x + 1, y + i + 1].astype(jnp.float32)
            lat[x + 1, y + i + 1] = (old + gelu(response)).astype(jnp.bfloat16)

    early = {}

    def inner_rows(some):
        for x in range(1, span_x - 1):
            for y in some:
                finish(x, y, product(x, y, 0, 3))
        for x, low, high in ((0, 1, 3), (span_x - 1, 0, 2)):
            for y in some:
                early[x, y] = product(x, y, low, high)

    inner_rows(range(2, span_y - 2, 2))
    land(0, (6, 7))
    inner_rows((0, span_y - 2))
    land(2, (0, 1))
    theirs = [weights(near_place.at[1 - k]) for k in (0, 1)]
    land(0, (0, 1))
    turn(0, edge[0, :, 0])
    turn(span_x + 1, edge[1, :, 0])

    def outer_rows(some):
        for y in some:
            for x, a in ((0, 0), (span_x - 1, 2)):
                finish(x, y, early[x, y] + product(x, y, a, a + 1))

    outer_rows(range(2, span_y - 2, 2))
    land(0, range(2, 6))
    outer_rows((0, span_y - 2))
    start(1, range(2, 8))

    def sample(of_weights, x, weight, low, high):
        weight_y, weight_z = of_weights[1:]
        part = dot(lat[x, low:high].reshape((high - low) * channels, span_z), weight_z)
        inner = None
        for y in range(low, high):
            term = part[(y - low) * channels:(y - low + 1) * channels] * weight_y[y]
            inner = term if inner is None else inner + term
        return inner * weight

    for k, x, weight in ((0, span_x, 0), (1, 1, span_x + 1)):
        weight_x = theirs[k][0][weight]
        partial[k] = sample(theirs[k], x, weight_x, 1, span_y + 1).astype(jnp.bfloat16)
        start(1, (k,))

    outbox[...] = jnp.zeros(outbox.shape, jnp.float32)
    weight_x, weight_y, weight_z = own_weights
    total = None
    for x in range(1, span_x + 1):
        term = sample(own_weights, x, weight_x[x], 1, span_y + 1)
        total = term if total is None else total + term
    land(1, range(2, 8))
    for y in (0, span_y + 1):
        part = dot(lat[:, y].reshape((span_x + 2) * channels, span_z), weight_z)
        inner = part[:channels] * weight_x[0]
        for x in range(1, span_x + 2):
            inner = inner + part[x * channels:(x + 1) * channels] * weight_x[x]
        total = total + inner * weight_y[y]
    for load in loads[3:]:
        load.wait()
    land(1, (0, 1))
    total = total + incoming[0].astype(jnp.float32) + incoming[1].astype(jnp.float32)
    row = jnp.concatenate([total.astype(jnp.bfloat16), attr[...]], axis=0)
    table = lax.dot_general(gather, row, NT, preferred_element_type=jnp.float32)
    table = table.astype(jnp.bfloat16)

    acts = [
        gelu(dot(table[s * half:(s + 1) * half], first_v[s])).astype(jnp.bfloat16) for s in range(2)
    ]
    for layer in range(middle_v.shape[1]):
        acts = [gelu(dot(acts[s], middle_v[s, layer])).astype(jnp.bfloat16) for s in range(2)]
    for s in range(2):
        value = lax.dot_general(last[s], acts[s], NT, preferred_element_type=jnp.float32)
        outbox[s, 0:value.shape[0], 0:half] = value

    def value_copy(j):
        other = lax.rem(me + j, peers)
        there = lax.rem(other, sects)
        return pltpu.make_async_remote_copy(
            src_ref=outbox.at[lax.div(there, sects // 2)],
            dst_ref=inbox.at[me],
            send_sem=value_send.at[j],
            recv_sem=value_recv.at[j],
            device_id={"brick": lax.div(other, sects), "sect": there},
            device_id_type=MESH,
        )

    for j in range(1, peers):
        value_copy(j).start()
    inbox[me] = outbox[lax.div(sect, sects // 2)]
    drain(0, range(8))
    drain(1, range(8))
    drain(2, (0, 1))
    for j in range(1, peers):
        value_copy(j).wait()

    width = inbox.shape[2]
    own = (brick * (sects // 2) + sect % (sects // 2)) * cap
    rolled = pltpu.roll(inbox[...].reshape(peers * 8, width), lax.rem(width - own, width), 1)
    for i in range(peers):
        out[:, i * cap:(i + 1) * cap] = rolled[i * 8:i * 8 + out.shape[0], 0:cap]


def on_device(
    sizes,
    geometry,
    conv_kernels,
    point_place,
    point_attr,
    destination,
    dense_first,
    dense_middle,
    dense_last,
):
    bricks, sects, slabs = sizes
    channels, span_x, span_y, span_z = geometry.shape
    count = point_place.shape[1]
    peers = bricks * sects
    cap = 5 * count // (4 * peers)
    width = -(-(peers // 2 * cap) // 128) * 128
    padded = (span_x + 2, span_y + 2, channels, span_z)
    attr = point_attr.T
    target = destination.reshape(1, count)
    return pl.pallas_call(
        functools.partial(kernel, bricks, sects, slabs),
        out_shape=pltpu.VMEM((dense_last.shape[1], peers * cap), jnp.float32),
        in_specs=[pl.BlockSpec(memory_space=pl.ANY)] * 8,
        out_specs=pl.BlockSpec(memory_space=pltpu.VMEM),
        scratch_shapes=[
            pltpu.VMEM(geometry.shape, jnp.bfloat16),
            pltpu.VMEM(((span_x + 2) * channels * span_y, span_z), jnp.float32),
            pltpu.VMEM(padded, jnp.bfloat16),
            pltpu.VMEM(padded, jnp.bfloat16),
            pltpu.VMEM(conv_kernels.shape, jnp.bfloat16),
            pltpu.VMEM((3 * channels, 9 * channels), jnp.bfloat16),
            pltpu.VMEM(point_place.shape, jnp.float32),
            pltpu.VMEM(attr.shape, jnp.bfloat16),
            pltpu.VMEM(target.shape, jnp.int32),
            pltpu.VMEM(dense_first.shape, jnp.bfloat16),
            pltpu.VMEM(dense_middle.shape, jnp.bfloat16),
            pltpu.VMEM(dense_last.shape, jnp.bfloat16),
            pltpu.VMEM((2,) + point_place.shape, jnp.float32),
            pltpu.VMEM((2, channels, count), jnp.bfloat16),
            pltpu.VMEM((2, channels, count), jnp.bfloat16),
            pltpu.VMEM((2, channels, 1, span_y, span_z), jnp.bfloat16),
            pltpu.VMEM((2, 8, width), jnp.float32),
            pltpu.VMEM((peers, 8, width), jnp.float32),
            pltpu.SemaphoreType.DMA((8 + span_x,)),
            pltpu.SemaphoreType.DMA((3, 8)),
            pltpu.SemaphoreType.DMA((3, 8)),
            pltpu.SemaphoreType.DMA((peers,)),
            pltpu.SemaphoreType.DMA((peers,)),
        ],
        compiler_params=pltpu.CompilerParams(
            collective_id=0, has_side_effects=True, vmem_limit_bytes=60 * 2**20
        ),
    )(
        geometry,
        conv_kernels,
        point_place,
        attr,
        target,
        dense_first,
        dense_middle,
        dense_last,
    )


def solution(mesh):
    sizes = tuple(mesh.shape[axis] for axis in ("brick", "sect", "slab"))
    in_specs = (
        P(None, ("case", "brick"), ("sect", "slab"), None),
        P(),
        P(None, ("case", "brick", "sect", "slab")),
        P(("case", "brick", "sect", "slab"), None),
        P(("case", "brick", "sect", "slab"), None),
        P(),
        P(),
        P(),
    )
    out_specs = P(None, ("case", "brick", "sect", "slab"))
    return jax.shard_map(
        functools.partial(on_device, sizes),
        mesh=mesh,
        in_specs=in_specs,
        out_specs=out_specs,
        check_vma=False,
    )
```
